32 devices in a mesh: seq: 8 (over y, x, core), dp: 4 (over z).
Axes of the slice: x: 2, y: 2, z: 4, core: 2. Of those that a mesh axis runs over, the one named last changes fastest.
Arguments:
- queries: bfloat16 [4, 4096, 1024], P('dp', 'seq'), may hold values from -6 to 6
- key_rows: bfloat16 [4, 4096, 1024], P('dp', 'seq'), may hold values from -6 to 6
- value_rows: bfloat16 [4, 4096, 1024], P('dp', 'seq'), may hold values from -6 to 6
- gate_rows: bfloat16 [4, 4096, 1024], P('dp', 'seq'), may hold values from -6 to 6
- cotangent: bfloat16 [4, 4096, 1024], P('dp', 'seq'), may hold values from -6 to 6
- far_blocks: int32 [4, 32, 4], P('dp'), may hold values from 0 to 31, as said below
- treated: int32 [4, 32], P('dp'), may hold values 0 or 1
- norm_gain: float32 [1024], replicated, may hold values from 0.1 to 1.9
- out_weight: bfloat16 [1024, 1024], replicated, may hold values from -0.1875 to 0.1875
Outputs:
- output: bfloat16 [4, 4096, 1024], P('dp', 'seq')
- grad_queries: bfloat16 [4, 4096, 1024], P('dp', 'seq')
- grad_keys: bfloat16 [4, 4096, 1024], P('dp', 'seq')
- grad_values: bfloat16 [4, 4096, 1024], P('dp', 'seq')
- grad_gate: bfloat16 [4, 4096, 1024], P('dp', 'seq')
- grad_weight: float32 [1024, 1024], P(('seq', 'dp'))
- grad_gain: float32 [1024], replicated
The draws below stay inside these ranges and needn't reach their ends.
Inputs may be any that keep to these rules, and one draw needn't show every extreme that they name: `far_blocks`: every entry names a block of the same history that is held by another index of seq than its query block. Of the 16 entries of the query blocks held by index s of seq, 3 name blocks of index (s + o) mod 8 for o = 1 and o = 2, and 2 for each other o from 3 to 7; which entries these are, and which block of that index, are drawn.
All inputs are finite; a program needn't handle non-finite values. No bound on the sum of `treated` on one device may be relied on, other than what follows from the above.
Results may differ from the reference program's by a relative error of at most 0.0065.
Values may be sent and summed in bfloat16 or wider, within the bound.
A program may use at most 192 MiB of HBM per device.

```python
import jax
import jax.numpy as jnp
from jax import lax

HEADS = 8
HEAD_DIM = 128
D = 1024
BLK = 128
FAR = 4
NB_DEV = 4
NBLK = 32
TOKENS = 4096
BATCH = 4


def draw_far_blocks(key, part):
    seq_count = NBLK // NB_DEV
    requests = NB_DEV * FAR

    def one_device(device_key, device):
        positions = jax.random.permutation(jax.random.fold_in(device_key, 1), requests)
        source = (device + 1 + positions % (seq_count - 1)) % seq_count
        inner = jax.random.randint(jax.random.fold_in(device_key, 3), (requests,), 0, NB_DEV)
        return (source * NB_DEV + inner).astype(jnp.int32).reshape(NB_DEV, FAR)

    def one_history(history_key):
        device_keys = jax.random.split(history_key, seq_count)
        listed = jax.vmap(one_device)(device_keys, jnp.arange(seq_count, dtype=jnp.int32))
        return listed.reshape(NBLK, FAR)
    return jax.vmap(one_history)(jax.random.split(jax.random.fold_in(key, 7), BATCH))


def plant(values, key, low, largest):
    extent = values.shape
    index_at = [jax.random.randint(jax.random.fold_in(key, axis), (), 0, extent[axis]) for axis in range(len(extent))]
    values = values.at[tuple(index_at)].set(low)
    longest = extent.index(max(extent))
    index_at[longest] = (index_at[longest] + 1) % extent[longest]
    return values.at[tuple(index_at)].set(largest)


def raised(values, stream_key, source, target, parts, factor):
    owner, partner = [(jnp.arange(values.shape[position]) // (values.shape[position] // parts)).reshape([-1 if axis == position else 1 for axis in range(values.ndim)]) for position in (source, target)]
    chosen = jax.random.permutation(stream_key, parts)[partner]
    strong = (owner == chosen) | (owner == (partner + parts // 2) % parts)
    return jnp.where(strong, factor * values, values)


def level_of(stream_key, extent, cuts, least, high):
    def one(axis_at, parts):
        heights = jax.random.uniform(jax.random.fold_in(jax.random.fold_in(stream_key, 6), axis_at), (parts,), jnp.float32, least / len(cuts), high / len(cuts))
        return jnp.repeat(jnp.exp(heights), extent[axis_at] // parts).reshape((-1,) + (1,) * (len(extent) - axis_at - 1))

    loudness = one(*cuts[0])
    for cut in cuts[1:]:
        loudness = loudness * one(*cut)
    return loudness


def noise(key, dims, width, most, cuts=(), kind=jnp.bfloat16):
    array = width * jax.random.normal(key, dims, jnp.float32)
    if cuts:
        array = array * level_of(key, dims, cuts, -0.22, 0.18)
    return jnp.clip(array, -most, most).astype(kind)


def heavy_noise(stream_key, extent, scale, limit, cuts, heavy, held_as=jnp.bfloat16):
    values = scale * jax.random.normal(stream_key, extent, jnp.float32)
    if cuts:
        values = values * level_of(stream_key, extent, cuts, -0.22, 0.18)
    return jnp.clip(raised(values, jax.random.fold_in(stream_key, 3), *heavy), -limit, limit).astype(held_as)


def setup_inputs(seed: int = 0) -> dict:
    streams_of = jax.random.split(jax.random.key(seed), 10)
    return {
        "queries": noise(streams_of[0], (BATCH, TOKENS, D), 1.0, 6.0, ((0, 4), (1, 8))),
        "key_rows": noise(streams_of[1], (BATCH, TOKENS, D), 1.0, 6.0, ((0, 4), (1, 8))),
        "value_rows": noise(streams_of[2], (BATCH, TOKENS, D), 1.0, 6.0, ((0, 4), (1, 8))),
        "gate_rows": heavy_noise(streams_of[3], (BATCH, TOKENS, D), 1.0, 6.0, ((0, 4), (1, 8)), (1, 2, 8, 2.0)),
        "cotangent": noise(streams_of[4], (BATCH, TOKENS, D), 1.0, 6.0, ((0, 4), (1, 8))),
        "far_blocks": draw_far_blocks(jax.random.fold_in(streams_of[9], 71), 0),
        "treated": plant((jax.random.randint(streams_of[6], (BATCH, NBLK), 0, 3) < 2).astype(jnp.int32), jax.random.fold_in(streams_of[6], 1), 0, 1),
        "norm_gain": jnp.clip(1.0 + 0.18 * jax.random.normal(streams_of[7], (D,), jnp.float32), 0.1, 1.9),
        "out_weight": noise(streams_of[8], (D, D), D ** -0.5, 0.1875),
    }


epsilon = 1e-05

def to_heads(rows):
    return rows.reshape(rows.shape[:-1] + (HEADS, HEAD_DIM))

def rounded(values):
    return lax.optimization_barrier(values.astype(jnp.bfloat16)).astype(jnp.float32)

def pair_scores(query_part, key_part):
    scores = jnp.einsum('pqhd,pkhd->phqk', to_heads(query_part).astype(jnp.float32), to_heads(key_part).astype(jnp.float32))
    return scores * HEAD_DIM ** (-0.5)

def pair_forward(query_part, key_part, value_part, pair_mask):
    weights = (jax.nn.silu(pair_scores(query_part, key_part)) * pair_mask[:, None]).astype(jnp.bfloat16)
    result = jnp.einsum('phqk,pkhd->pqhd', weights.astype(jnp.float32), to_heads(value_part).astype(jnp.float32))
    return result.reshape(query_part.shape)

def pair_backward(query_part, key_part, value_part, grad_part, pair_mask):
    scores = pair_scores(query_part, key_part)
    logistic = jax.nn.sigmoid(scores)
    weights = (jax.nn.silu(scores) * pair_mask[:, None]).astype(jnp.bfloat16)
    grad_heads = to_heads(grad_part).astype(jnp.float32)
    grad_weights = jnp.einsum('pqhd,pkhd->phqk', grad_heads, to_heads(value_part).astype(jnp.float32))
    grad_value = jnp.einsum('phqk,pqhd->pkhd', weights.astype(jnp.float32), grad_heads)
    grad_scores = (grad_weights * logistic * (1.0 + scores * (1.0 - logistic)) * pair_mask[:, None] * HEAD_DIM ** (-0.5)).astype(jnp.bfloat16)
    grad_query = jnp.einsum('phqk,pkhd->pqhd', grad_scores.astype(jnp.float32), to_heads(key_part).astype(jnp.float32))
    grad_key = jnp.einsum('phqk,pqhd->pkhd', grad_scores.astype(jnp.float32), to_heads(query_part).astype(jnp.float32))
    row_shape = query_part.shape
    return (grad_query.reshape(row_shape), grad_key.reshape(row_shape), grad_value.reshape(row_shape))

def one_sequence(items, norm_gain, out_weight):
    queries, key_rows, value_rows, gate_rows, cotangent, far_blocks, treated = items
    query_blocks = queries.reshape(NBLK, BLK, D)
    key_blocks = key_rows.reshape(NBLK, BLK, D)
    value_blocks = value_rows.reshape(NBLK, BLK, D)
    zero_block = jnp.zeros((1, BLK, D), jnp.bfloat16)
    prev_keys = jnp.concatenate([zero_block, key_blocks[:-1]], axis=0)
    prev_values = jnp.concatenate([zero_block, value_blocks[:-1]], axis=0)
    causal = jnp.tril(jnp.ones((BLK, BLK), jnp.float32))[None]
    all_ones = jnp.ones((1, BLK, BLK), jnp.float32)
    flat_far = far_blocks.reshape(NBLK * FAR).astype(jnp.int32)
    far_keys = key_blocks[flat_far]
    far_values = value_blocks[flat_far]
    far_queries = jnp.repeat(query_blocks, FAR, axis=0)
    far_mask = treated[flat_far].astype(jnp.float32)[:, None, None]
    far_out = rounded(pair_forward(far_queries, far_keys, far_values, far_mask)).reshape(NBLK, FAR, BLK, D).sum(axis=1)
    attention = pair_forward(query_blocks, key_blocks, value_blocks, causal)
    attention = attention + pair_forward(query_blocks, prev_keys, prev_values, all_ones) + far_out
    attention = attention.reshape(TOKENS, D)
    centered = attention - lax.optimization_barrier(jnp.mean(attention, axis=1, keepdims=True))
    inv_std = lax.rsqrt(lax.optimization_barrier(jnp.mean(centered * centered, axis=1, keepdims=True)) + epsilon)
    normed = centered * inv_std
    gate_vals = gate_rows.astype(jnp.float32)
    mixed = (normed * norm_gain * gate_vals).astype(jnp.bfloat16)
    output = jnp.dot(mixed, out_weight, preferred_element_type=jnp.float32).astype(jnp.bfloat16)
    grad_mixed = jnp.dot(cotangent, out_weight.T, preferred_element_type=jnp.float32)
    weight_part = jnp.dot(mixed.T, cotangent, preferred_element_type=jnp.float32)
    grad_gate = (grad_mixed * normed * norm_gain).astype(jnp.bfloat16)
    scaled = grad_mixed * gate_vals
    gain_part = lax.optimization_barrier(jnp.sum(scaled * normed, axis=0))
    grad_hat = scaled * norm_gain
    grad_attn = inv_std * (grad_hat - lax.optimization_barrier(jnp.mean(grad_hat, axis=1, keepdims=True)) - normed * lax.optimization_barrier(jnp.mean(grad_hat * normed, axis=1, keepdims=True)))
    grad_blocks = grad_attn.astype(jnp.bfloat16).reshape(NBLK, BLK, D)
    dq_diag, dk_diag, dv_diag = pair_backward(query_blocks, key_blocks, value_blocks, grad_blocks, causal)
    dq_prev, dk_prev, dv_prev = pair_backward(query_blocks, prev_keys, prev_values, grad_blocks, all_ones)
    zero_terms = jnp.zeros((1, BLK, D), jnp.float32)
    next_keys = jnp.concatenate([rounded(dk_prev[1:]), zero_terms], axis=0)
    next_values = jnp.concatenate([rounded(dv_prev[1:]), zero_terms], axis=0)
    far_grads = jnp.repeat(grad_blocks, FAR, axis=0)
    dq_far, dk_far, dv_far = pair_backward(far_queries, far_keys, far_values, far_grads, far_mask)
    far_query = rounded(dq_far).reshape(NBLK, FAR, BLK, D).sum(axis=1)
    far_key = jax.ops.segment_sum(rounded(dk_far), flat_far, num_segments=NBLK)
    far_value = jax.ops.segment_sum(rounded(dv_far), flat_far, num_segments=NBLK)
    grad_queries = (dq_diag + dq_prev + far_query).astype(jnp.bfloat16).reshape(TOKENS, D)
    grad_keys = (dk_diag + next_keys + far_key).astype(jnp.bfloat16).reshape(TOKENS, D)
    grad_values = (dv_diag + next_values + far_value).astype(jnp.bfloat16).reshape(TOKENS, D)
    return (output, grad_queries, grad_keys, grad_values, grad_gate, weight_part, gain_part)

def reference(queries, key_rows, value_rows, gate_rows, cotangent, far_blocks, treated, norm_gain, out_weight):

    def per_sequence(items):
        return one_sequence(items, norm_gain, out_weight)
    results = lax.map(per_sequence, (queries, key_rows, value_rows, gate_rows, cotangent, far_blocks, treated))
    output, grad_queries, grad_keys, grad_values, grad_gate, weight_parts, gain_parts = results
    return (output, grad_queries, grad_keys, grad_values, grad_gate, lax.optimization_barrier(jnp.sum(weight_parts, axis=0)), lax.optimization_barrier(jnp.sum(gain_parts, axis=0)))
```

```python
import functools

import jax
import jax.numpy as jnp
from jax import lax
from jax.experimental import pallas as pl
from jax.experimental.pallas import tpu as pltpu
from jax.sharding import PartitionSpec as P

HEADS = 8
HEAD_DIM = 128
BLK = 128
FAR = 4
EPS = 1e-05
SCALE = HEAD_DIM ** (-0.5)
NT = (((1,), (1,)), ((), ()))
TN = (((0,), (0,)), ((), ()))


def dot(a, b, dims=(((1,), (0,)), ((), ()))):
    return lax.dot_general(a, b, dims, preferred_element_type=jnp.float32)


def silu_parts(raw):
    half = raw * (0.5 * SCALE)
    t = jnp.tanh(half)
    act = half + half * t
    sig = 0.5 + 0.5 * t
    return act, sig + act * (1.0 - sig)


def query_kernel(
    nb, far_s, treated_s, my_s, q_ref, k0, v0, k1, v1, k2, v2, k3, v3, k4, v4, k5, v5,
    gate_ref, cot_ref, gain_ref, w_ref,
    out_ref, dq_ref, dgate_ref, mixed_ref, c_ref, dgain_ref, att, slope,
):
    i = pl.program_id(0)
    block = my_s[0] * nb + i
    keys = (k0, k1, k2, k3, k4, k5)
    vals = (v0, v1, v2, v3, v4, v5)
    flags = [None, (block > 0).astype(jnp.float32)]
    flags += [treated_s[far_s[block * FAR + f]].astype(jnp.float32) for f in range(FAR)]
    row = lax.broadcasted_iota(jnp.int32, (BLK, BLK), 0)
    col = lax.broadcasted_iota(jnp.int32, (BLK, BLK), 1)
    tril = (row >= col).astype(jnp.float32)
    for h in range(HEADS):
        hs = slice(h * HEAD_DIM, (h + 1) * HEAD_DIM)
        q = q_ref[:, hs]
        acts = []
        for p in range(2 + FAR):
            act, der = silu_parts(dot(q, keys[p][:, hs], NT))
            m = tril if p == 0 else flags[p]
            acts.append((act * m).astype(jnp.bfloat16))
            slope[h, :, p * BLK : (p + 1) * BLK] = der * m
        att[:, hs] = dot(
            jnp.concatenate(acts, axis=1), jnp.concatenate([v[:, hs] for v in vals], axis=0)
        )
    attention = att[...]
    centered = attention - jnp.mean(attention, axis=1, keepdims=True)
    inv_std = lax.rsqrt(jnp.mean(centered * centered, axis=1, keepdims=True) + EPS)
    normed = centered * inv_std
    gate = gate_ref[...].astype(jnp.float32)
    gain = gain_ref[...]
    mixed = (normed * gain * gate).astype(jnp.bfloat16)
    mixed_ref[...] = mixed
    out_ref[...] = dot(mixed, w_ref[...]).astype(jnp.bfloat16)
    gm = dot(cot_ref[...], w_ref[...], NT)
    dgate_ref[...] = (gm * normed * gain).astype(jnp.bfloat16)
    scaled = gm * gate
    part = jnp.sum(scaled * normed, axis=0, keepdims=True)

    @pl.when(i == 0)
    def _():
        dgain_ref[...] = part

    @pl.when(i > 0)
    def _():
        dgain_ref[...] += part

    g = scaled * gain
    c = inv_std * (
        g - jnp.mean(g, axis=1, keepdims=True)
        - normed * jnp.mean(g * normed, axis=1, keepdims=True)
    )
    c_ref[...] = c.astype(jnp.bfloat16)
    for h in range(HEADS):
        hs = slice(h * HEAD_DIM, (h + 1) * HEAD_DIM)
        ch = c_ref[:, hs]
        ds = []
        for p in range(2 + FAR):
            da = dot(ch, vals[p][:, hs], NT)
            ds.append((da * slope[h, :, p * BLK : (p + 1) * BLK]).astype(jnp.bfloat16))
        dq = dot(
            jnp.concatenate(ds, axis=1), jnp.concatenate([k[:, hs] for k in keys], axis=0)
        )
        dq_ref[:, hs] = (dq * SCALE).astype(jnp.bfloat16)


def key_kernel(
    steps, qi_s, ki_s, on_s, q_ref, c_ref, k_ref, v_ref, dk_ref, dv_ref, dk_acc, dv_acc
):
    r = pl.program_id(0)

    @pl.when(r == 0)
    def _():
        dk_acc[...] = jnp.zeros_like(dk_acc)
        dv_acc[...] = jnp.zeros_like(dv_acc)

    at = pl.ds(pl.multiple_of(ki_s[r] * BLK, BLK), BLK)
    mode = on_s[r]
    on = (mode > 0).astype(jnp.float32)
    off_diag = jnp.where(mode == 2, 0.0, on)
    row = lax.broadcasted_iota(jnp.int32, (BLK, BLK), 0)
    col = lax.broadcasted_iota(jnp.int32, (BLK, BLK), 1)
    m = jnp.where(col >= row, on, off_diag)
    for h in range(HEADS):
        hs = slice(h * HEAD_DIM, (h + 1) * HEAD_DIM)
        q = q_ref[:, hs]
        c = c_ref[:, hs]
        act, der = silu_parts(dot(k_ref[at, hs], q, NT))
        da = dot(v_ref[at, hs], c, NT)
        dv_acc[at, hs] += dot((act * m).astype(jnp.bfloat16), c)
        dk_acc[at, hs] += dot((da * der * m).astype(jnp.bfloat16), q)

    @pl.when(r == steps - 1)
    def _():
        dk_ref[...] = (dk_acc[...] * SCALE).astype(jnp.bfloat16)
        dv_ref[...] = dv_acc[...].astype(jnp.bfloat16)


def run_query(q, k, v, k_all, v_all, gate, cot, far, treated, me, gain, w):
    rows, width = q.shape
    nb = rows // BLK
    shape = (BLK, width)
    own = pl.BlockSpec(shape, lambda i, far, tr, my: (i, 0))
    prev = pl.BlockSpec(shape, lambda i, far, tr, my: (jnp.maximum(my[0] * nb + i - 1, 0), 0))

    def listed(f):
        return pl.BlockSpec(shape, lambda i, far, tr, my: (far[(my[0] * nb + i) * FAR + f], 0))

    kv_specs = [own, own, prev, prev]
    kv = [k, v, k_all, v_all]
    for f in range(FAR):
        kv_specs += [listed(f)] * 2
        kv += [k_all, v_all]
    whole = pl.BlockSpec((width, width), lambda i, far, tr, my: (0, 0))
    vec = pl.BlockSpec((1, width), lambda i, far, tr, my: (0, 0))
    big = jax.ShapeDtypeStruct((rows, width), jnp.bfloat16)
    return pl.pallas_call(
        functools.partial(query_kernel, nb),
        out_shape=(big, big, big, big, big, jax.ShapeDtypeStruct((1, width), jnp.float32)),
        grid_spec=pltpu.PrefetchScalarGridSpec(
            num_scalar_prefetch=3,
            grid=(nb,),
            in_specs=[own] + kv_specs + [own, own, vec, whole],
            out_specs=(own, own, own, own, own, vec),
            scratch_shapes=[
                pltpu.VMEM((BLK, width), jnp.float32),
                pltpu.VMEM((HEADS, BLK, (2 + FAR) * BLK), jnp.float32),
            ],
        ),
        compiler_params=pltpu.CompilerParams(vmem_limit_bytes=40 * 2**20),
        cost_estimate=pl.CostEstimate(
            flops=8 * 10**9, bytes_accessed=24 * 2**20, transcendentals=3 * 10**6
        ),
        name="query_side",
    )(far, treated, me, q, *kv, gate, cot, gain, w)


def run_keys(qi, ki, on, q_all, c_all, k, v):
    rows, width = k.shape
    steps = qi.shape[0]
    pick = pl.BlockSpec((BLK, width), lambda r, qi, ki, on: (qi[r], 0))
    whole = pl.BlockSpec((rows, width), lambda r, qi, ki, on: (0, 0))
    big = jax.ShapeDtypeStruct((rows, width), jnp.bfloat16)
    return pl.pallas_call(
        functools.partial(key_kernel, steps),
        out_shape=(big, big),
        grid_spec=pltpu.PrefetchScalarGridSpec(
            num_scalar_prefetch=3,
            grid=(steps,),
            in_specs=[pick, pick, whole, whole],
            out_specs=(whole, whole),
            scratch_shapes=[pltpu.VMEM((rows, width), jnp.float32)] * 2,
        ),
        compiler_params=pltpu.CompilerParams(vmem_limit_bytes=40 * 2**20),
        cost_estimate=pl.CostEstimate(
            flops=4 * 10**9, bytes_accessed=16 * 2**20, transcendentals=3 * 10**6
        ),
        name="key_side",
    )(qi, ki, on, q_all, c_all, k, v)


def key_plan(far, treated, me, nb):
    total = far.shape[0]
    mine = (far // nb) == me
    ids = jnp.arange(total)
    rank = jnp.sum((ids[None, :] < ids[:, None]) & mine[None, :], axis=1)
    hit = mine[None, :] & (rank[None, :] == jnp.arange(nb * FAR)[:, None])
    flag = jnp.sum(
        jnp.where(far[:, None] == jnp.arange(treated.shape[0])[None, :], treated[None, :], 0),
        axis=1,
    )

    def take(values):
        return jnp.sum(jnp.where(hit, values[None, :], 0), axis=1)

    local = jnp.arange(nb)
    after = me * nb + local + 1
    last = treated.shape[0] - 1
    qi = jnp.concatenate([me * nb + local, jnp.minimum(after, last), take(ids // FAR)])
    ki = jnp.concatenate([local, local, take(far % nb)])
    on = jnp.concatenate(
        [jnp.full((nb,), 2), (after <= last).astype(jnp.int32), take(flag)]
    )
    return qi.astype(jnp.int32), ki.astype(jnp.int32), on.astype(jnp.int32)


def gather(rows):
    return lax.all_gather(rows, "seq", axis=0, tiled=True)


def body(q, k, v, gate, cot, far_blocks, treated, gain, w):
    q, k, v, gate, cot = q[0], k[0], v[0], gate[0], cot[0]
    rows, width = q.shape
    nb = rows // BLK
    me = lax.axis_index("seq").astype(jnp.int32)
    far = far_blocks[0].reshape(-1)
    flags = treated[0]
    k_all, v_all = gather(k), gather(v)
    q_all = gather(q)
    out, dq, dgate, mixed, c, dgain = run_query(
        q, k, v, k_all, v_all, gate, cot, far, flags, me[None], gain[None], w
    )
    c_all = gather(c)
    grad_weight = dot(mixed, cot, TN)
    seqs, dps = lax.axis_size("seq"), lax.axis_size("dp")
    grad_weight = grad_weight.reshape(seqs, dps, -1, width)
    grad_weight = lax.psum_scatter(grad_weight, "dp", scatter_dimension=1, tiled=False)
    grad_weight = lax.psum_scatter(grad_weight, "seq", scatter_dimension=0, tiled=False)
    dgain = lax.psum(dgain[0], ("seq", "dp"))
    qi, ki, on = key_plan(far, flags, me, nb)
    dk, dv = run_keys(qi, ki, on, q_all, c_all, k, v)
    return out[None], dq[None], dk[None], dv[None], dgate[None], grad_weight, dgain


def solution(mesh):
    big = P("dp", "seq", None)
    in_specs = (big,) * 5 + (P("dp", None, None), P("dp", None), P(), P())
    out_specs = (big,) * 5 + (P(("seq", "dp"), None), P())
    return jax.shard_map(body, mesh=mesh, in_specs=in_specs, out_specs=out_specs, check_vma=False)
```

```python
import functools

import jax
import jax.numpy as jnp
from jax import lax
from jax.experimental import pallas as pl
from jax.experimental.pallas import tpu as pltpu
from jax.sharding import PartitionSpec as P

HEADS = 8
HEAD_DIM = 128
BLK = 128
FAR = 4
EPS = 1e-05
CHUNKS = 4
SEQS, DPS = 8, 4
SCALE = HEAD_DIM ** (-0.5)
NT = (((1,), (1,)), ((), ()))
TN = (((0,), (0,)), ((), ()))


def dot(a, b, dims=(((1,), (0,)), ((), ()))):
    return lax.dot_general(a, b, dims, preferred_element_type=jnp.float32)


def silu_parts(raw):
    half = raw * (0.5 * SCALE)
    t = jnp.tanh(half)
    act = half + half * t
    sig = 0.5 + 0.5 * t
    return act, sig + act * (1.0 - sig)


def query_kernel(
    nb, far_s, treated_s, my_s, q_ref, k0, v0, k1, v1, k2, v2, k3, v3, k4, v4, k5, v5,
    gate_ref, cot_ref, gain_ref, w_ref,
    out_ref, dq_ref, dgate_ref, mixed_ref, c_ref, dgain_ref, att, slope,
):
    i = pl.program_id(0)
    block = my_s[0] * nb + i
    keys = (k0, k1, k2, k3, k4, k5)
    vals = (v0, v1, v2, v3, v4, v5)
    flags = [None, (block > 0).astype(jnp.float32)]
    flags += [treated_s[far_s[block * FAR + f]].astype(jnp.float32) for f in range(FAR)]
    row = lax.broadcasted_iota(jnp.int32, (BLK, BLK), 0)
    col = lax.broadcasted_iota(jnp.int32, (BLK, BLK), 1)
    tril = (row >= col).astype(jnp.float32)
    for h in range(HEADS):
        hs = slice(h * HEAD_DIM, (h + 1) * HEAD_DIM)
        q = q_ref[:, hs]
        acts = []
        for p in range(2 + FAR):
            act, der = silu_parts(dot(q, keys[p][:, hs], NT))
            m = tril if p == 0 else flags[p]
            acts.append((act * m).astype(jnp.bfloat16))
            slope[h, :, p * BLK : (p + 1) * BLK] = der * m
        att[:, hs] = dot(
            jnp.concatenate(acts, axis=1), jnp.concatenate([v[:, hs] for v in vals], axis=0)
        )
    attention = att[...]
    centered = attention - jnp.mean(attention, axis=1, keepdims=True)
    inv_std = lax.rsqrt(jnp.mean(centered * centered, axis=1, keepdims=True) + EPS)
    normed = centered * inv_std
    gate = gate_ref[...].astype(jnp.float32)
    gain = gain_ref[...]
    mixed = (normed * gain * gate).astype(jnp.bfloat16)
    mixed_ref[...] = mixed
    out_ref[...] = dot(mixed, w_ref[...]).astype(jnp.bfloat16)
    gm = dot(cot_ref[...], w_ref[...], NT)
    dgate_ref[...] = (gm * normed * gain).astype(jnp.bfloat16)
    scaled = gm * gate
    part = jnp.sum((scaled * normed).reshape(BLK // 8, 8, -1), axis=0)

    @pl.when(i == 0)
    def _():
        dgain_ref[...] = part

    @pl.when(i > 0)
    def _():
        dgain_ref[...] += part

    g = scaled * gain
    c = inv_std * (
        g - jnp.mean(g, axis=1, keepdims=True)
        - normed * jnp.mean(g * normed, axis=1, keepdims=True)
    )
    c_ref[...] = c.astype(jnp.bfloat16)
    for h in range(HEADS):
        hs = slice(h * HEAD_DIM, (h + 1) * HEAD_DIM)
        ch = c_ref[:, hs]
        ds = []
        for p in range(2 + FAR):
            da = dot(ch, vals[p][:, hs], NT)
            ds.append((da * slope[h, :, p * BLK : (p + 1) * BLK]).astype(jnp.bfloat16))
        dq = dot(
            jnp.concatenate(ds, axis=1), jnp.concatenate([k[:, hs] for k in keys], axis=0)
        )
        dq_ref[:, hs] = (dq * SCALE).astype(jnp.bfloat16)


def key_kernel(
    steps, qi_s, ki_s, on_s, q_ref, c_ref, k_ref, v_ref, dk_ref, dv_ref, dk_acc, dv_acc
):
    r = pl.program_id(0)

    @pl.when(r == 0)
    def _():
        dk_acc[...] = jnp.zeros_like(dk_acc)
        dv_acc[...] = jnp.zeros_like(dv_acc)

    at = pl.ds(pl.multiple_of(ki_s[r] * BLK, BLK), BLK)
    mode = on_s[r]
    on = (mode > 0).astype(jnp.float32)
    off_diag = jnp.where(mode == 2, 0.0, on)
    row = lax.broadcasted_iota(jnp.int32, (BLK, BLK), 0)
    col = lax.broadcasted_iota(jnp.int32, (BLK, BLK), 1)
    m = jnp.where(col >= row, on, off_diag)
    for h in range(HEADS):
        hs = slice(h * HEAD_DIM, (h + 1) * HEAD_DIM)
        q = q_ref[:, hs]
        c = c_ref[:, hs]
        act, der = silu_parts(dot(k_ref[at, hs], q, NT))
        da = dot(v_ref[at, hs], c, NT)
        dv_acc[at, hs] += dot((act * m).astype(jnp.bfloat16), c)
        dk_acc[at, hs] += dot((da * der * m).astype(jnp.bfloat16), q)

    @pl.when(r == steps - 1)
    def _():
        dk_ref[...] = (dk_acc[...] * SCALE).astype(jnp.bfloat16)
        dv_ref[...] = dv_acc[...].astype(jnp.bfloat16)


def run_query(q, k, v, k_all, v_all, gate, cot, far, treated, me, gain, w):
    rows, width = q.shape
    nb = rows // BLK
    shape = (BLK, width)
    own = pl.BlockSpec(shape, lambda i, far, tr, my: (i, 0))
    prev = pl.BlockSpec(shape, lambda i, far, tr, my: (jnp.maximum(my[0] * nb + i - 1, 0), 0))

    def listed(f):
        return pl.BlockSpec(shape, lambda i, far, tr, my: (far[(my[0] * nb + i) * FAR + f], 0))

    kv_specs = [own, own, prev, prev]
    kv = [k, v, k_all, v_all]
    for f in range(FAR):
        kv_specs += [listed(f)] * 2
        kv += [k_all, v_all]
    whole = pl.BlockSpec((width, width), lambda i, far, tr, my: (0, 0))
    vec = pl.BlockSpec((1, width), lambda i, far, tr, my: (0, 0))
    vec8 = pl.BlockSpec((8, width), lambda i, far, tr, my: (0, 0))
    big = jax.ShapeDtypeStruct((rows, width), jnp.bfloat16)
    return pl.pallas_call(
        functools.partial(query_kernel, nb),
        out_shape=(big, big, big, big, big, jax.ShapeDtypeStruct((8, width), jnp.float32)),
        grid_spec=pltpu.PrefetchScalarGridSpec(
            num_scalar_prefetch=3,
            grid=(nb,),
            in_specs=[own] + kv_specs + [own, own, vec, whole],
            out_specs=(own, own, own, own, own, vec8),
            scratch_shapes=[
                pltpu.VMEM((BLK, width), jnp.float32),
                pltpu.VMEM((HEADS, BLK, (2 + FAR) * BLK), jnp.float32),
            ],
        ),
        compiler_params=pltpu.CompilerParams(vmem_limit_bytes=40 * 2**20),
        cost_estimate=pl.CostEstimate(
            flops=8 * 10**9, bytes_accessed=24 * 2**20, transcendentals=3 * 10**6
        ),
        name="query_side",
    )(far, treated, me, q, *kv, gate, cot, gain, w)


def run_keys(qi, ki, on, q_all, c_all, k, v):
    rows, width = k.shape
    steps = qi.shape[0]
    pick = pl.BlockSpec((BLK, width), lambda r, qi, ki, on: (qi[r], 0))
    whole = pl.BlockSpec((rows, width), lambda r, qi, ki, on: (0, 0))
    big = jax.ShapeDtypeStruct((rows, width), jnp.bfloat16)
    return pl.pallas_call(
        functools.partial(key_kernel, steps),
        out_shape=(big, big),
        grid_spec=pltpu.PrefetchScalarGridSpec(
            num_scalar_prefetch=3,
            grid=(steps,),
            in_specs=[pick, pick, whole, whole],
            out_specs=(whole, whole),
            scratch_shapes=[pltpu.VMEM((rows, width), jnp.float32)] * 2,
        ),
        compiler_params=pltpu.CompilerParams(vmem_limit_bytes=40 * 2**20),
        cost_estimate=pl.CostEstimate(
            flops=4 * 10**9, bytes_accessed=16 * 2**20, transcendentals=3 * 10**6
        ),
        name="key_side",
    )(qi, ki, on, q_all, c_all, k, v)


def key_plan(far, treated, me, nb):
    total = far.shape[0]
    mine = (far // nb) == me
    ids = jnp.arange(total)
    rank = jnp.sum((ids[None, :] < ids[:, None]) & mine[None, :], axis=1)
    hit = mine[None, :] & (rank[None, :] == jnp.arange(nb * FAR)[:, None])
    flag = jnp.sum(
        jnp.where(far[:, None] == jnp.arange(treated.shape[0])[None, :], treated[None, :], 0),
        axis=1,
    )

    def take(values):
        return jnp.sum(jnp.where(hit, values[None, :], 0), axis=1)

    local = jnp.arange(nb)
    after = me * nb + local + 1
    last = treated.shape[0] - 1
    qi = jnp.concatenate([me * nb + local, jnp.minimum(after, last), take(ids // FAR)])
    ki = jnp.concatenate([local, local, take(far % nb)])
    on = jnp.concatenate(
        [jnp.full((nb,), 2), (after <= last).astype(jnp.int32), take(flag)]
    )
    return qi.astype(jnp.int32), ki.astype(jnp.int32), on.astype(jnp.int32)


def places():
    me = lax.axis_index("seq")
    x, y = (me // 2) % 2, (me // 4) % 2
    side = me + 1 - 2 * (me % 2)
    over_x = 2 - 4 * x
    over_y = 4 - 8 * y
    return me, side, me + over_x, me + over_y, me + over_x + over_y


def greet(peers):
    barrier = pltpu.get_barrier_semaphore()
    for peer in peers:
        pl.semaphore_signal(barrier, inc=1, device_id=peer, device_id_type=pl.DeviceIdType.MESH)
    pl.semaphore_wait(barrier, len(peers))


class Spread:
    def __init__(self, src, dst, send, recv, own):
        self.src, self.dst, self.send, self.recv, self.own = src, dst, send, recv, own
        self.me, self.side, self.px, self.py, self.pd = places()
        self.rows = src.shape[0]
        self.step = self.rows // CHUNKS
        self.sent = []

    def slot(self, origin, j):
        return self.dst.at[pl.ds(pl.multiple_of(origin * self.rows, self.rows) + j * self.step, self.step)]

    def copy(self, src, origin, kind, j, to):
        return pltpu.make_async_remote_copy(
            src_ref=src,
            dst_ref=self.slot(origin, j),
            send_sem=self.send.at[kind, j],
            recv_sem=self.recv.at[kind, j],
            device_id={"seq": to},
            device_id_type=pl.DeviceIdType.MESH,
        )

    def push(self, src, origin, kind, j, to):
        made = self.copy(src, origin, kind, j, to)
        made.start()
        self.sent.append(made)

    def take(self, origin, kind, j):
        self.copy(self.slot(origin, j), origin, kind, j, self.side).wait_recv()

    def begin(self):
        self.keep = pltpu.make_async_copy(
            self.src,
            self.dst.at[pl.ds(pl.multiple_of(self.me * self.rows, self.rows), self.rows)],
            self.own,
        )
        half = CHUNKS // 2
        for n in range(CHUNKS):
            j, i = n, (n + half) % CHUNKS
            self.push(self.src.at[pl.ds(j * self.step, self.step)], self.me, 0, j, self.px)
            self.push(self.src.at[pl.ds(i * self.step, self.step)], self.me, 1, i, self.py)
        for j in range(CHUNKS):
            self.push(self.src.at[pl.ds(j * self.step, self.step)], self.me, 3, j, self.side)
        self.keep.start()

    def relay(self):
        half = CHUNKS // 2
        for n in range(CHUNKS):
            j, i = n, (n + half) % CHUNKS
            self.take(self.px, 0, j)
            if n < half:
                self.push(self.slot(self.px, j), self.px, 2, j, self.py)
            self.push(self.slot(self.px, j), self.px, 4, j, self.side)
            self.take(self.py, 1, i)
            if n < half:
                self.push(self.slot(self.py, i), self.py, 2, i, self.px)
            self.push(self.slot(self.py, i), self.py, 5, i, self.side)

    def finish(self):
        half = CHUNKS // 2
        for n in range(half):
            for j in (n, n + half):
                self.take(self.pd, 2, j)
                self.push(self.slot(self.pd, j), self.pd, 6, j, self.side)

    def drain(self):
        far = self.side - self.me
        for kind, origin in ((3, self.me), (4, self.px), (5, self.py), (6, self.pd)):
            for j in range(CHUNKS):
                self.take(origin + far, kind, j)
        for made in self.sent:
            made.wait_send()
        self.keep.wait()


def seq_peers():
    _, side, px, py, pd = places()
    return [{"seq": p} for p in (side, px, py, pd)]


def spread_kernel(count, *refs):
    srcs, dsts = refs[:count], refs[count : 2 * count]
    send, recv, own = refs[2 * count :]
    greet(seq_peers())
    jobs = [
        Spread(srcs[a], dsts[a], send.at[a], recv.at[a], own.at[a]) for a in range(count)
    ]
    for job in jobs:
        job.begin()
    for job in jobs:
        job.relay()
    for job in jobs:
        job.finish()
    for job in jobs:
        job.drain()


def spread(arrays, ident):
    count = len(arrays)
    rows, width = arrays[0].shape
    anywhere = pl.BlockSpec(memory_space=pl.ANY)
    full = jax.ShapeDtypeStruct((SEQS * rows, width), jnp.bfloat16)
    return pl.pallas_call(
        functools.partial(spread_kernel, count),
        out_shape=(full,) * count,
        in_specs=[anywhere] * count,
        out_specs=(anywhere,) * count,
        scratch_shapes=[
            pltpu.SemaphoreType.DMA((count, 7, CHUNKS)),
            pltpu.SemaphoreType.DMA((count, 7, CHUNKS)),
            pltpu.SemaphoreType.DMA((count,)),
        ],
        compiler_params=pltpu.CompilerParams(collective_id=ident, has_side_effects=True),
        name="spread_rows",
    )(*arrays)


def tail_kernel(
    c_ref, gw_ref, dg_ref, c_all, gw_out, dg_out,
    got_side, mid, got_z, low, got_xy, dg_side, dg_z, dg_yx,
    send, recv, own, red_send, red_recv,
):
    greet(seq_peers() + [{"dp": lax.rem(lax.axis_index("dp") + k, DPS)} for k in range(1, DPS)])
    me, side, px, py, pd = places()
    core = me % 2
    z = lax.axis_index("dp")
    yx = me // 2
    job = Spread(c_ref, c_all, send, recv, own)
    sent = []

    def push(src, dst, at, to):
        made = pltpu.make_async_remote_copy(
            src_ref=src, dst_ref=dst, send_sem=red_send.at[at], recv_sem=red_recv.at[at],
            device_id=to, device_id_type=pl.DeviceIdType.MESH,
        )
        made.start()
        sent.append(made)
        return made

    one = push(gw_ref.at[1 - core], got_side, 0, {"seq": side})
    dg_one = push(dg_ref, dg_side, 1, {"seq": side})
    job.begin()
    one.wait_recv()
    dg_one.wait_recv()
    for p in range(DPS):
        mid[p] = (
            gw_ref[core, p].astype(jnp.float32) + got_side[p].astype(jnp.float32)
        ).astype(jnp.bfloat16)
    dg_z[z] = dg_ref[...] + dg_side[...]
    twos = []
    for k in range(1, DPS):
        to = lax.rem(z + k, DPS)
        twos.append(push(mid.at[to], got_z.at[k - 1], 2 * k, {"dp": to}))
        twos.append(push(dg_z.at[z], dg_z.at[z], 2 * k + 1, {"dp": to}))
    job.relay()
    for two in twos:
        two.wait_recv()
    total = gw_ref[core, z].astype(jnp.float32) + got_side[z].astype(jnp.float32)
    for k in range(DPS - 1):
        total += got_z[k].astype(jnp.float32)
    low[...] = total.astype(jnp.bfloat16).reshape(low.shape)
    dg_yx[yx] = dg_z[0] + dg_z[1] + dg_z[2] + dg_z[3]
    threes = []
    for k, to in enumerate((px, py, pd)):
        threes.append(push(low.at[to // 2], got_xy.at[k], 8 + 2 * k, {"seq": to}))
        threes.append(push(dg_yx.at[yx], dg_yx.at[yx], 9 + 2 * k, {"seq": to}))
    job.finish()
    for three in threes:
        three.wait_recv()
    result = low[yx].astype(jnp.float32)
    for k in range(3):
        result += got_xy[k].astype(jnp.float32)
    gw_out[...] = result
    dg_out[...] = dg_yx[0] + dg_yx[1] + dg_yx[2] + dg_yx[3]
    job.drain()
    for made in sent:
        made.wait_send()


def tail(c, gw, dg):
    rows, width = c.shape
    depth = width // (SEQS * DPS)
    anywhere = pl.BlockSpec(memory_space=pl.ANY)
    vmem = pl.BlockSpec(memory_space=pltpu.VMEM)
    part = (SEQS // 2) * depth
    b16 = jnp.bfloat16
    return pl.pallas_call(
        tail_kernel,
        out_shape=(
            jax.ShapeDtypeStruct((SEQS * rows, width), b16),
            jax.ShapeDtypeStruct((depth, width), jnp.float32),
            jax.ShapeDtypeStruct(dg.shape, jnp.float32),
        ),
        in_specs=[anywhere, vmem, vmem],
        out_specs=(anywhere, vmem, vmem),
        scratch_shapes=[
            pltpu.VMEM((DPS, part, width), b16),
            pltpu.VMEM((DPS, part, width), b16),
            pltpu.VMEM((DPS - 1, part, width), b16),
            pltpu.VMEM((SEQS // 2, depth, width), b16),
            pltpu.VMEM((3, depth, width), b16),
            pltpu.VMEM(dg.shape, jnp.float32),
            pltpu.VMEM((DPS,) + dg.shape, jnp.float32),
            pltpu.VMEM((SEQS // 2,) + dg.shape, jnp.float32),
            pltpu.SemaphoreType.DMA((7, CHUNKS)),
            pltpu.SemaphoreType.DMA((7, CHUNKS)),
            pltpu.SemaphoreType.DMA,
            pltpu.SemaphoreType.DMA((14,)),
            pltpu.SemaphoreType.DMA((14,)),
        ],
        compiler_params=pltpu.CompilerParams(
            collective_id=2, has_side_effects=True, vmem_limit_bytes=40 * 2**20
        ),
        name="tail_exchange",
    )(c, gw, dg)


def gather(rows):
    return lax.all_gather(rows, "seq", axis=0, tiled=True)


def body(q, k, v, gate, cot, far_blocks, treated, gain, w):
    q, k, v, gate, cot = q[0], k[0], v[0], gate[0], cot[0]
    rows, width = q.shape
    nb = rows // BLK
    me = lax.axis_index("seq").astype(jnp.int32)
    far = far_blocks[0].reshape(-1)
    flags = treated[0]
    seqs, dps = lax.axis_size("seq"), lax.axis_size("dp")
    direct = (seqs, dps) == (SEQS, DPS)
    if direct:
        k_all, v_all = spread([k, v], 1)
        q_late, k_all, v_all = lax.optimization_barrier((q, k_all, v_all))
        q_all = gather(q_late)
    else:
        k_all, v_all, q_all = gather(k), gather(v), gather(q)
    out, dq, dgate, mixed, c, dgain = run_query(
        q, k, v, k_all, v_all, gate, cot, far, flags, me[None], gain[None], w
    )
    grad_weight = dot(mixed, cot, TN)
    if direct:
        parts = grad_weight.astype(jnp.bfloat16).reshape(seqs // 2, 2, dps, -1, width)
        parts = parts.transpose(1, 2, 0, 3, 4).reshape(2, dps, -1, width)
        c_all, grad_weight, dgain = tail(c, parts, dgain)
        dgain = jnp.sum(dgain, axis=0)
    else:
        c_all = gather(c)
        grad_weight = lax.psum_scatter(grad_weight, ("seq", "dp"), scatter_dimension=0, tiled=True)
        dgain = lax.psum(jnp.sum(dgain, axis=0), ("seq", "dp"))
    qi, ki, on = key_plan(far, flags, me, nb)
    dk, dv = run_keys(qi, ki, on, q_all, c_all, k, v)
    return out[None], dq[None], dk[None], dv[None], dgate[None], grad_weight, dgain


def solution(mesh):
    big = P("dp", "seq", None)
    in_specs = (big,) * 5 + (P("dp", None, None), P("dp", None), P(), P())
    out_specs = (big,) * 5 + (P(("seq", "dp"), None), P())
    return jax.shard_map(body, mesh=mesh, in_specs=in_specs, out_specs=out_specs, check_vma=False)
```

```python
import functools

import jax
import jax.numpy as jnp
from jax import lax
from jax.experimental import pallas as pl
from jax.experimental.pallas import tpu as pltpu
from jax.sharding import PartitionSpec as P

HEADS = 8
HEAD_DIM = 128
BLK = 128
FAR = 4
EPS = 1e-05
CHUNKS = 4
SEQS, DPS = 8, 4
SCALE = HEAD_DIM ** (-0.5)
NT = (((1,), (1,)), ((), ()))
TN = (((0,), (0,)), ((), ()))


def dot(a, b, dims=(((1,), (0,)), ((), ()))):
    return lax.dot_general(a, b, dims, preferred_element_type=jnp.float32)


def silu_parts(raw):
    half = raw * (0.5 * SCALE)
    t = jnp.tanh(half)
    act = half + half * t
    sig = 0.5 + 0.5 * t
    return act, sig + act * (1.0 - sig)


def query_kernel(
    nb, far_s, treated_s, my_s, q_ref, k0, v0, k1, v1, k2, v2, k3, v3, k4, v4, k5, v5,
    gate_ref, cot_ref, gain_ref, w_ref,
    out_ref, dq_ref, dgate_ref, mixed_ref, c_ref, dgain_ref, att, slope, vals, keys,
):
    i = pl.program_id(0)
    block = my_s[0] * nb + i
    flags = [None, (block > 0).astype(jnp.float32)]
    flags += [treated_s[far_s[block * FAR + f]].astype(jnp.float32) for f in range(FAR)]
    for p, (one_k, one_v) in enumerate(zip((k0, k1, k2, k3, k4, k5), (v0, v1, v2, v3, v4, v5))):
        at = slice(p * BLK, (p + 1) * BLK)
        keys[at] = one_k[...]
        vals[at] = one_v[...] if p == 0 else one_v[...] * flags[p].astype(jnp.bfloat16)
    row = lax.broadcasted_iota(jnp.int32, (BLK, BLK), 0)
    col = lax.broadcasted_iota(jnp.int32, (BLK, BLK), 1)
    tril = (row >= col).astype(jnp.float32)
    for h in range(HEADS):
        hs = slice(h * HEAD_DIM, (h + 1) * HEAD_DIM)
        q = q_ref[:, hs]
        act, der = silu_parts(dot(q, keys[:, hs], NT))
        act = jnp.concatenate([act[:, :BLK] * tril, act[:, BLK:]], axis=1)
        slope[h, :, :BLK] = der[:, :BLK] * tril
        slope[h, :, BLK:] = der[:, BLK:]
        att[:, hs] = dot(act.astype(jnp.bfloat16), vals[:, hs])
    attention = att[...]
    centered = attention - jnp.mean(attention, axis=1, keepdims=True)
    inv_std = lax.rsqrt(jnp.mean(centered * centered, axis=1, keepdims=True) + EPS)
    normed = centered * inv_std
    gate = gate_ref[...].astype(jnp.float32)
    gain = gain_ref[...]
    mixed = (normed * gain * gate).astype(jnp.bfloat16)
    mixed_ref[...] = mixed
    out_ref[...] = dot(mixed, w_ref[...]).astype(jnp.bfloat16)
    gm = dot(cot_ref[...], w_ref[...], NT)
    dgate_ref[...] = (gm * normed * gain).astype(jnp.bfloat16)
    scaled = gm * gate
    part = jnp.sum((scaled * normed).reshape(BLK // 8, 8, -1), axis=0)

    @pl.when(i == 0)
    def _():
        dgain_ref[...] = part

    @pl.when(i > 0)
    def _():
        dgain_ref[...] += part

    g = scaled * gain
    c = inv_std * (
        g - jnp.mean(g, axis=1, keepdims=True)
        - normed * jnp.mean(g * normed, axis=1, keepdims=True)
    )
    c_ref[...] = c.astype(jnp.bfloat16)
    for h in range(HEADS):
        hs = slice(h * HEAD_DIM, (h + 1) * HEAD_DIM)
        ch = c_ref[:, hs]
        ds = dot(ch, vals[:, hs], NT) * slope[h]
        dq = dot(ds.astype(jnp.bfloat16), keys[:, hs])
        dq_ref[:, hs] = (dq * SCALE).astype(jnp.bfloat16)


def key_kernel(nb, steps, qi_s, ki_s, on_s, *refs):
    q_refs, c_refs = refs[:nb], refs[nb : 2 * nb]
    k_ref, v_ref, dk_ref, dv_ref, dk_acc, dv_acc = refs[2 * nb :]
    r = pl.program_id(0)
    row = lax.broadcasted_iota(jnp.int32, (BLK, BLK), 0)
    col = lax.broadcasted_iota(jnp.int32, (BLK, BLK), 1)
    upper = (col >= row).astype(jnp.float32)

    @pl.when(r == 0)
    def _():
        for n in range(nb):
            at = slice(n * BLK, (n + 1) * BLK)
            for h in range(HEADS):
                hs = slice(h * HEAD_DIM, (h + 1) * HEAD_DIM)
                q, c = q_refs[n][:, hs], c_refs[n][:, hs]
                act, der = silu_parts(dot(k_ref[at, hs], q, NT))
                da = dot(v_ref[at, hs], c, NT)
                dv_acc[at, hs] = dot((act * upper).astype(jnp.bfloat16), c)
                dk_acc[at, hs] = dot((da * der * upper).astype(jnp.bfloat16), q)

    @pl.when(r > 0)
    def _():
        for n in range(nb):
            at = pl.ds(pl.multiple_of(ki_s[r * nb + n] * BLK, BLK), BLK)
            on = (on_s[r * nb + n] > 0).astype(jnp.bfloat16)
            for h in range(HEADS):
                hs = slice(h * HEAD_DIM, (h + 1) * HEAD_DIM)
                q, c = q_refs[n][:, hs], c_refs[n][:, hs] * on
                act, der = silu_parts(dot(k_ref[at, hs], q, NT))
                da = dot(v_ref[at, hs], c, NT)
                dv_acc[at, hs] += dot(act.astype(jnp.bfloat16), c)
                dk_acc[at, hs] += dot((da * der).astype(jnp.bfloat16), q)

    @pl.when(r == steps - 1)
    def _():
        dk_ref[...] = (dk_acc[...] * SCALE).astype(jnp.bfloat16)
        dv_ref[...] = dv_acc[...].astype(jnp.bfloat16)


def run_query(q, k, v, k_all, v_all, gate, cot, far, treated, me, gain, w):
    rows, width = q.shape
    nb = rows // BLK
    shape = (BLK, width)
    own = pl.BlockSpec(shape, lambda i, far, tr, my: (i, 0))
    prev = pl.BlockSpec(shape, lambda i, far, tr, my: (jnp.maximum(my[0] * nb + i - 1, 0), 0))

    def listed(f):
        return pl.BlockSpec(shape, lambda i, far, tr, my: (far[(my[0] * nb + i) * FAR + f], 0))

    kv_specs = [own, own, prev, prev]
    kv = [k, v, k_all, v_all]
    for f in range(FAR):
        kv_specs += [listed(f)] * 2
        kv += [k_all, v_all]
    whole = pl.BlockSpec((width, width), lambda i, far, tr, my: (0, 0))
    vec = pl.BlockSpec((1, width), lambda i, far, tr, my: (0, 0))
    vec8 = pl.BlockSpec((8, width), lambda i, far, tr, my: (0, 0))
    big = jax.ShapeDtypeStruct((rows, width), jnp.bfloat16)
    return pl.pallas_call(
        functools.partial(query_kernel, nb),
        out_shape=(big, big, big, big, big, jax.ShapeDtypeStruct((8, width), jnp.float32)),
        grid_spec=pltpu.PrefetchScalarGridSpec(
            num_scalar_prefetch=3,
            grid=(nb,),
            in_specs=[own] + kv_specs + [own, own, vec, whole],
            out_specs=(own, own, own, own, own, vec8),
            scratch_shapes=[
                pltpu.VMEM((BLK, width), jnp.float32),
                pltpu.VMEM((HEADS, BLK, (2 + FAR) * BLK), jnp.float32),
                pltpu.VMEM(((2 + FAR) * BLK, width), jnp.bfloat16),
                pltpu.VMEM(((2 + FAR) * BLK, width), jnp.bfloat16),
            ],
        ),
        compiler_params=pltpu.CompilerParams(vmem_limit_bytes=60 * 2**20),
        cost_estimate=pl.CostEstimate(
            flops=8 * 10**9, bytes_accessed=24 * 2**20, transcendentals=3 * 10**6
        ),
        name="query_side",
    )(far, treated, me, q, *kv, gate, cot, gain, w)


def run_keys(qi, ki, on, q_all, c_all, k, v):
    rows, width = k.shape
    nb = rows // BLK
    steps = qi.shape[0] // nb

    def pick(n):
        return pl.BlockSpec((BLK, width), lambda r, qi, ki, on: (qi[r * nb + n], 0))

    picks = [pick(n) for n in range(nb)]
    whole = pl.BlockSpec((rows, width), lambda r, qi, ki, on: (0, 0))
    big = jax.ShapeDtypeStruct((rows, width), jnp.bfloat16)
    return pl.pallas_call(
        functools.partial(key_kernel, nb, steps),
        out_shape=(big, big),
        grid_spec=pltpu.PrefetchScalarGridSpec(
            num_scalar_prefetch=3,
            grid=(steps,),
            in_specs=picks + picks + [whole, whole],
            out_specs=(whole, whole),
            scratch_shapes=[pltpu.VMEM((rows, width), jnp.float32)] * 2,
        ),
        compiler_params=pltpu.CompilerParams(vmem_limit_bytes=60 * 2**20),
        cost_estimate=pl.CostEstimate(
            flops=4 * 10**9, bytes_accessed=16 * 2**20, transcendentals=3 * 10**6
        ),
        name="key_side",
    )(qi, ki, on, *[q_all] * nb, *[c_all] * nb, k, v)


def key_plan(far, treated, me, nb):
    total = far.shape[0]
    mine = (far // nb) == me
    ids = jnp.arange(total)
    rank = jnp.sum((ids[None, :] < ids[:, None]) & mine[None, :], axis=1)
    hit = mine[None, :] & (rank[None, :] == jnp.arange(nb * FAR)[:, None])
    flag = jnp.sum(
        jnp.where(far[:, None] == jnp.arange(treated.shape[0])[None, :], treated[None, :], 0),
        axis=1,
    )

    def take(values):
        return jnp.sum(jnp.where(hit, values[None, :], 0), axis=1)

    local = jnp.arange(nb)
    after = me * nb + local + 1
    last = treated.shape[0] - 1
    qi = jnp.concatenate([me * nb + local, jnp.minimum(after, last), take(ids // FAR)])
    ki = jnp.concatenate([local, local, take(far % nb)])
    on = jnp.concatenate(
        [jnp.full((nb,), 2), (after <= last).astype(jnp.int32), take(flag)]
    )
    return qi.astype(jnp.int32), ki.astype(jnp.int32), on.astype(jnp.int32)


def places():
    me = lax.axis_index("seq")
    x, y = (me // 2) % 2, (me // 4) % 2
    side = me + 1 - 2 * (me % 2)
    over_x = 2 - 4 * x
    over_y = 4 - 8 * y
    return me, side, me + over_x, me + over_y, me + over_x + over_y


def greet(peers):
    barrier = pltpu.get_barrier_semaphore()
    for peer in peers:
        pl.semaphore_signal(barrier, inc=1, device_id=peer, device_id_type=pl.DeviceIdType.MESH)
    pl.semaphore_wait(barrier, len(peers))


class Spread:
    def __init__(self, src, dst, send, recv, own):
        self.src, self.dst, self.send, self.recv, self.own = src, dst, send, recv, own
        self.me, self.side, self.px, self.py, self.pd = places()
        self.rows = src.shape[0]
        self.step = self.rows // CHUNKS
        self.sent = []

    def slot(self, origin, j):
        return self.dst.at[pl.ds(pl.multiple_of(origin * self.rows, self.rows) + j * self.step, self.step)]

    def copy(self, src, origin, kind, j, to):
        return pltpu.make_async_remote_copy(
            src_ref=src,
            dst_ref=self.slot(origin, j),
            send_sem=self.send.at[kind, j],
            recv_sem=self.recv.at[kind, j],
            device_id={"seq": to},
            device_id_type=pl.DeviceIdType.MESH,
        )

    def push(self, src, origin, kind, j, to):
        made = self.copy(src, origin, kind, j, to)
        made.start()
        self.sent.append(made)

    def take(self, origin, kind, j):
        self.copy(self.slot(origin, j), origin, kind, j, self.side).wait_recv()

    def begin(self):
        self.keep = pltpu.make_async_copy(
            self.src,
            self.dst.at[pl.ds(pl.multiple_of(self.me * self.rows, self.rows), self.rows)],
            self.own,
        )
        half = CHUNKS // 2
        for n in range(CHUNKS):
            j, i = n, (n + half) % CHUNKS
            self.push(self.src.at[pl.ds(j * self.step, self.step)], self.me, 0, j, self.px)
            self.push(self.src.at[pl.ds(i * self.step, self.step)], self.me, 1, i, self.py)
        for j in range(CHUNKS):
            self.push(self.src.at[pl.ds(j * self.step, self.step)], self.me, 3, j, self.side)
        self.keep.start()

    def relay(self):
        half = CHUNKS // 2
        for n in range(CHUNKS):
            j, i = n, (n + half) % CHUNKS
            self.take(self.px, 0, j)
            if n < half:
                self.push(self.slot(self.px, j), self.px, 2, j, self.py)
            self.push(self.slot(self.px, j), self.px, 4, j, self.side)
            self.take(self.py, 1, i)
            if n < half:
                self.push(self.slot(self.py, i), self.py, 2, i, self.px)
            self.push(self.slot(self.py, i), self.py, 5, i, self.side)

    def finish(self):
        half = CHUNKS // 2
        for n in range(half):
            for j in (n, n + half):
                self.take(self.pd, 2, j)
                self.push(self.slot(self.pd, j), self.pd, 6, j, self.side)

    def drain(self):
        far = self.side - self.me
        for kind, origin in ((3, self.me), (4, self.px), (5, self.py), (6, self.pd)):
            for j in range(CHUNKS):
                self.take(origin + far, kind, j)
        for made in self.sent:
            made.wait_send()
        self.keep.wait()


def seq_peers():
    _, side, px, py, pd = places()
    return [{"seq": p} for p in (side, px, py, pd)]


def spread_kernel(count, *refs):
    srcs, dsts = refs[:count], refs[count : 2 * count]
    send, recv, own = refs[2 * count :]
    greet(seq_peers())
    jobs = [
        Spread(srcs[a], dsts[a], send.at[a], recv.at[a], own.at[a]) for a in range(count)
    ]
    for job in jobs:
        job.begin()
    for job in jobs:
        job.relay()
    for job in jobs:
        job.finish()
    for job in jobs:
        job.drain()


def spread(arrays, ident):
    count = len(arrays)
    rows, width = arrays[0].shape
    anywhere = pl.BlockSpec(memory_space=pl.ANY)
    full = jax.ShapeDtypeStruct((SEQS * rows, width), jnp.bfloat16)
    return pl.pallas_call(
        functools.partial(spread_kernel, count),
        out_shape=(full,) * count,
        in_specs=[anywhere] * count,
        out_specs=(anywhere,) * count,
        scratch_shapes=[
            pltpu.SemaphoreType.DMA((count, 7, CHUNKS)),
            pltpu.SemaphoreType.DMA((count, 7, CHUNKS)),
            pltpu.SemaphoreType.DMA((count,)),
        ],
        compiler_params=pltpu.CompilerParams(collective_id=ident, has_side_effects=True, vmem_limit_bytes=60 * 2**20),
        name="spread_rows",
    )(*arrays)


def tail_kernel(
    c_ref, gw_ref, dg_ref, c_all, gw_out, dg_out,
    got_side, mid, got_z, low, got_xy, dg_side, dg_z, dg_yx,
    send, recv, own, red_send, red_recv,
):
    greet(seq_peers() + [{"dp": lax.rem(lax.axis_index("dp") + k, DPS)} for k in range(1, DPS)])
    me, side, px, py, pd = places()
    core = me % 2
    z = lax.axis_index("dp")
    yx = me // 2
    job = Spread(c_ref, c_all, send, recv, own)
    sent = []

    def push(src, dst, at, to):
        made = pltpu.make_async_remote_copy(
            src_ref=src, dst_ref=dst, send_sem=red_send.at[at], recv_sem=red_recv.at[at],
            device_id=to, device_id_type=pl.DeviceIdType.MESH,
        )
        made.start()
        sent.append(made)
        return made

    one = push(gw_ref.at[1 - core], got_side, 0, {"seq": side})
    dg_one = push(dg_ref, dg_side, 1, {"seq": side})
    job.begin()
    one.wait_recv()
    dg_one.wait_recv()
    for p in range(DPS):
        mid[p] = (
            gw_ref[core, p].astype(jnp.float32) + got_side[p].astype(jnp.float32)
        ).astype(jnp.bfloat16)
    dg_z[z] = dg_ref[...] + dg_side[...]
    twos = []
    for k in range(1, DPS):
        to = lax.rem(z + k, DPS)
        twos.append(push(mid.at[to], got_z.at[k - 1], 2 * k, {"dp": to}))
        twos.append(push(dg_z.at[z], dg_z.at[z], 2 * k + 1, {"dp": to}))
    job.relay()
    for two in twos:
        two.wait_recv()
    total = gw_ref[core, z].astype(jnp.float32) + got_side[z].astype(jnp.float32)
    for k in range(DPS - 1):
        total += got_z[k].astype(jnp.float32)
    low[...] = total.astype(jnp.bfloat16).reshape(low.shape)
    dg_yx[yx] = dg_z[0] + dg_z[1] + dg_z[2] + dg_z[3]
    threes = []
    for k, to in enumerate((px, py, pd)):
        threes.append(push(low.at[to // 2], got_xy.at[k], 8 + 2 * k, {"seq": to}))
        threes.append(push(dg_yx.at[yx], dg_yx.at[yx], 9 + 2 * k, {"seq": to}))
    job.finish()
    for three in threes:
        three.wait_recv()
    result = low[yx].astype(jnp.float32)
    for k in range(3):
        result += got_xy[k].astype(jnp.float32)
    gw_out[...] = result
    dg_out[...] = dg_yx[0] + dg_yx[1] + dg_yx[2] + dg_yx[3]
    job.drain()
    for made in sent:
        made.wait_send()


def tail(c, gw, dg):
    rows, width = c.shape
    depth = width // (SEQS * DPS)
    anywhere = pl.BlockSpec(memory_space=pl.ANY)
    vmem = pl.BlockSpec(memory_space=pltpu.VMEM)
    part = (SEQS // 2) * depth
    b16 = jnp.bfloat16
    return pl.pallas_call(
        tail_kernel,
        out_shape=(
            jax.ShapeDtypeStruct((SEQS * rows, width), b16),
            jax.ShapeDtypeStruct((depth, width), jnp.float32),
            jax.ShapeDtypeStruct(dg.shape, jnp.float32),
        ),
        in_specs=[anywhere, vmem, vmem],
        out_specs=(anywhere, vmem, vmem),
        scratch_shapes=[
            pltpu.VMEM((DPS, part, width), b16),
            pltpu.VMEM((DPS, part, width), b16),
            pltpu.VMEM((DPS - 1, part, width), b16),
            pltpu.VMEM((SEQS // 2, depth, width), b16),
            pltpu.VMEM((3, depth, width), b16),
            pltpu.VMEM(dg.shape, jnp.float32),
            pltpu.VMEM((DPS,) + dg.shape, jnp.float32),
            pltpu.VMEM((SEQS // 2,) + dg.shape, jnp.float32),
            pltpu.SemaphoreType.DMA((7, CHUNKS)),
            pltpu.SemaphoreType.DMA((7, CHUNKS)),
            pltpu.SemaphoreType.DMA,
            pltpu.SemaphoreType.DMA((14,)),
            pltpu.SemaphoreType.DMA((14,)),
        ],
        compiler_params=pltpu.CompilerParams(
            collective_id=2, has_side_effects=True, vmem_limit_bytes=60 * 2**20
        ),
        name="tail_exchange",
    )(c, gw, dg)


def gather(rows):
    return lax.all_gather(rows, "seq", axis=0, tiled=True)


def body(q, k, v, gate, cot, far_blocks, treated, gain, w):
    q, k, v, gate, cot = q[0], k[0], v[0], gate[0], cot[0]
    rows, width = q.shape
    nb = rows // BLK
    me = lax.axis_index("seq").astype(jnp.int32)
    far = far_blocks[0].reshape(-1)
    flags = treated[0]
    seqs, dps = lax.axis_size("seq"), lax.axis_size("dp")
    direct = (seqs, dps) == (SEQS, DPS)
    if direct:
        k_all, v_all = spread([k, v], 1)
        q_late, k_all, v_all = lax.optimization_barrier((q, k_all, v_all))
        q_all = gather(q_late)
    else:
        k_all, v_all, q_all = gather(k), gather(v), gather(q)
    out, dq, dgate, mixed, c, dgain = run_query(
        q, k, v, k_all, v_all, gate, cot, far, flags, me[None], gain[None], w
    )
    grad_weight = dot(mixed, cot, TN)
    if direct:
        parts = grad_weight.astype(jnp.bfloat16).reshape(seqs // 2, 2, dps, -1, width)
        parts = parts.transpose(1, 2, 0, 3, 4).reshape(2, dps, -1, width)
        c_all, grad_weight, dgain = tail(c, parts, dgain)
        dgain = jnp.sum(dgain, axis=0)
    else:
        c_all = gather(c)
        grad_weight = lax.psum_scatter(grad_weight, ("seq", "dp"), scatter_dimension=0, tiled=True)
        dgain = lax.psum(jnp.sum(dgain, axis=0), ("seq", "dp"))
    qi, ki, on = key_plan(far, flags, me, nb)
    dk, dv = run_keys(qi, ki, on, q_all, c_all, k, v)
    return out[None], dq[None], dk[None], dv[None], dgate[None], grad_weight, dgain


def solution(mesh):
    big = P("dp", "seq", None)
    in_specs = (big,) * 5 + (P("dp", None, None), P("dp", None), P(), P())
    out_specs = (big,) * 5 + (P(("seq", "dp"), None), P())
    return jax.shard_map(body, mesh=mesh, in_specs=in_specs, out_specs=out_specs, check_vma=False)
```

```python
import functools

import jax
import jax.numpy as jnp
from jax import lax
from jax.experimental import pallas as pl
from jax.experimental.pallas import tpu as pltpu
from jax.sharding import PartitionSpec as P

HEADS = 8
HEAD_DIM = 128
BLK = 128
FAR = 4
EPS = 1e-05
CHUNKS = 4
GROUP = 4
SEQS, DPS = 8, 4
SCALE = HEAD_DIM ** (-0.5)
NT = (((1,), (1,)), ((), ()))
TN = (((0,), (0,)), ((), ()))


def dot(a, b, dims=(((1,), (0,)), ((), ()))):
    return lax.dot_general(a, b, dims, preferred_element_type=jnp.float32)


def silu_parts(raw):
    half = raw * (0.5 * SCALE)
    t = jnp.tanh(half)
    act = half + half * t
    sig = 0.5 + 0.5 * t
    return act, sig + act * (1.0 - sig)


def query_kernel(
    nb, far_s, treated_s, my_s, q_ref, k0, v0, k1, v1, k2, v2, k3, v3, k4, v4, k5, v5,
    gate_ref, cot_ref, gain_ref, w_ref,
    out_ref, dq_ref, dgate_ref, mixed_ref, c_ref, dgain_ref, att, slope, vals, keys,
):
    i = pl.program_id(0)
    block = my_s[0] * nb + i
    flags = [None, (block > 0).astype(jnp.float32)]
    flags += [treated_s[far_s[block * FAR + f]].astype(jnp.float32) for f in range(FAR)]
    for p, (one_k, one_v) in enumerate(zip((k0, k1, k2, k3, k4, k5), (v0, v1, v2, v3, v4, v5))):
        at = slice(p * BLK, (p + 1) * BLK)
        keys[at] = one_k[...]
        vals[at] = one_v[...] if p == 0 else one_v[...] * flags[p].astype(jnp.bfloat16)
    row = lax.broadcasted_iota(jnp.int32, (BLK, BLK), 0)
    col = lax.broadcasted_iota(jnp.int32, (BLK, BLK), 1)
    tril = (row >= col).astype(jnp.float32)
    for h in range(HEADS):
        hs = slice(h * HEAD_DIM, (h + 1) * HEAD_DIM)
        q = q_ref[:, hs]
        act, der = silu_parts(dot(q, keys[:, hs], NT))
        act = jnp.concatenate([act[:, :BLK] * tril, act[:, BLK:]], axis=1)
        slope[h, :, :BLK] = der[:, :BLK] * tril
        slope[h, :, BLK:] = der[:, BLK:]
        att[:, hs] = dot(act.astype(jnp.bfloat16), vals[:, hs])
    attention = att[...]
    centered = attention - jnp.mean(attention, axis=1, keepdims=True)
    inv_std = lax.rsqrt(jnp.mean(centered * centered, axis=1, keepdims=True) + EPS)
    normed = centered * inv_std
    gate = gate_ref[...].astype(jnp.float32)
    gain = gain_ref[...]
    mixed = (normed * gain * gate).astype(jnp.bfloat16)
    mixed_ref[...] = mixed
    out_ref[...] = dot(mixed, w_ref[...]).astype(jnp.bfloat16)
    gm = dot(cot_ref[...], w_ref[...], NT)
    dgate_ref[...] = (gm * normed * gain).astype(jnp.bfloat16)
    scaled = gm * gate
    part = jnp.sum((scaled * normed).reshape(BLK // 8, 8, -1), axis=0)

    @pl.when(i == 0)
    def _():
        dgain_ref[...] = part

    @pl.when(i > 0)
    def _():
        dgain_ref[...] += part

    g = scaled * gain
    c = inv_std * (
        g - jnp.mean(g, axis=1, keepdims=True)
        - normed * jnp.mean(g * normed, axis=1, keepdims=True)
    )
    c_ref[...] = c.astype(jnp.bfloat16)
    for h in range(HEADS):
        hs = slice(h * HEAD_DIM, (h + 1) * HEAD_DIM)
        ch = c_ref[:, hs]
        ds = dot(ch, vals[:, hs], NT) * slope[h]
        dq = dot(ds.astype(jnp.bfloat16), keys[:, hs])
        dq_ref[:, hs] = (dq * SCALE).astype(jnp.bfloat16)


def key_kernel(nb, steps, qi_s, ki_s, on_s, *refs):
    q_refs, c_refs = refs[:nb], refs[nb : 2 * nb]
    k_ref, v_ref, dk_ref, dv_ref, dk_acc, dv_acc = refs[2 * nb :]
    r = pl.program_id(0)
    row = lax.broadcasted_iota(jnp.int32, (BLK, BLK), 0)
    col = lax.broadcasted_iota(jnp.int32, (BLK, BLK), 1)
    upper = (col >= row).astype(jnp.float32)

    @pl.when(r == 0)
    def _():
        for n in range(nb):
            at = slice(n * BLK, (n + 1) * BLK)
            for h in range(HEADS):
                hs = slice(h * HEAD_DIM, (h + 1) * HEAD_DIM)
                q, c = q_refs[n][:, hs], c_refs[n][:, hs]
                act, der = silu_parts(dot(k_ref[at, hs], q, NT))
                da = dot(v_ref[at, hs], c, NT)
                dv_acc[at, hs] = dot((act * upper).astype(jnp.bfloat16), c)
                dk_acc[at, hs] = dot((da * der * upper).astype(jnp.bfloat16), q)

    @pl.when(r > 0)
    def _():
        for n in range(nb):
            at = pl.ds(pl.multiple_of(ki_s[r * nb + n] * BLK, BLK), BLK)
            on = (on_s[r * nb + n] > 0).astype(jnp.bfloat16)
            for first in range(0, HEADS, GROUP):
                cuts = [
                    slice(h * HEAD_DIM, (h + 1) * HEAD_DIM) for h in range(first, first + GROUP)
                ]
                qs = [q_refs[n][:, hs] for hs in cuts]
                cs = [c_refs[n][:, hs] * on for hs in cuts]
                raw = [dot(k_ref[at, hs], q, NT) for hs, q in zip(cuts, qs)]
                da = [dot(v_ref[at, hs], c, NT) for hs, c in zip(cuts, cs)]
                act, der = silu_parts(jnp.concatenate(raw, axis=1))
                ds = (jnp.concatenate(da, axis=1) * der).astype(jnp.bfloat16)
                act = act.astype(jnp.bfloat16)
                dv = [dot(act[:, g * BLK : (g + 1) * BLK], cs[g]) for g in range(GROUP)]
                dk = [dot(ds[:, g * BLK : (g + 1) * BLK], qs[g]) for g in range(GROUP)]
                wide = slice(first * HEAD_DIM, (first + GROUP) * HEAD_DIM)
                dv_acc[at, wide] += jnp.concatenate(dv, axis=1)
                dk_acc[at, wide] += jnp.concatenate(dk, axis=1)

    @pl.when(r == steps - 1)
    def _():
        dk_ref[...] = (dk_acc[...] * SCALE).astype(jnp.bfloat16)
        dv_ref[...] = dv_acc[...].astype(jnp.bfloat16)


def run_query(q, k, v, k_all, v_all, gate, cot, far, treated, me, gain, w):
    rows, width = q.shape
    nb = rows // BLK
    shape = (BLK, width)
    own = pl.BlockSpec(shape, lambda i, far, tr, my: (i, 0))
    prev = pl.BlockSpec(shape, lambda i, far, tr, my: (jnp.maximum(my[0] * nb + i - 1, 0), 0))

    def listed(f):
        return pl.BlockSpec(shape, lambda i, far, tr, my: (far[(my[0] * nb + i) * FAR + f], 0))

    kv_specs = [own, own, prev, prev]
    kv = [k, v, k_all, v_all]
    for f in range(FAR):
        kv_specs += [listed(f)] * 2
        kv += [k_all, v_all]
    whole = pl.BlockSpec((width, width), lambda i, far, tr, my: (0, 0))
    vec = pl.BlockSpec((1, width), lambda i, far, tr, my: (0, 0))
    vec8 = pl.BlockSpec((8, width), lambda i, far, tr, my: (0, 0))
    big = jax.ShapeDtypeStruct((rows, width), jnp.bfloat16)
    return pl.pallas_call(
        functools.partial(query_kernel, nb),
        out_shape=(big, big, big, big, big, jax.ShapeDtypeStruct((8, width), jnp.float32)),
        grid_spec=pltpu.PrefetchScalarGridSpec(
            num_scalar_prefetch=3,
            grid=(nb,),
            in_specs=[own] + kv_specs + [own, own, vec, whole],
            out_specs=(own, own, own, own, own, vec8),
            scratch_shapes=[
                pltpu.VMEM((BLK, width), jnp.float32),
                pltpu.VMEM((HEADS, BLK, (2 + FAR) * BLK), jnp.float32),
                pltpu.VMEM(((2 + FAR) * BLK, width), jnp.bfloat16),
                pltpu.VMEM(((2 + FAR) * BLK, width), jnp.bfloat16),
            ],
        ),
        compiler_params=pltpu.CompilerParams(vmem_limit_bytes=60 * 2**20),
        cost_estimate=pl.CostEstimate(
            flops=8 * 10**9, bytes_accessed=24 * 2**20, transcendentals=3 * 10**6
        ),
        name="query_side",
    )(far, treated, me, q, *kv, gate, cot, gain, w)


def run_keys(qi, ki, on, q_all, c_all, k, v):
    rows, width = k.shape
    nb = rows // BLK
    steps = qi.shape[0] // nb

    def pick(n):
        return pl.BlockSpec((BLK, width), lambda r, qi, ki, on: (qi[r * nb + n], 0))

    picks = [pick(n) for n in range(nb)]
    whole = pl.BlockSpec((rows, width), lambda r, qi, ki, on: (0, 0))
    big = jax.ShapeDtypeStruct((rows, width), jnp.bfloat16)
    return pl.pallas_call(
        functools.partial(key_kernel, nb, steps),
        out_shape=(big, big),
        grid_spec=pltpu.PrefetchScalarGridSpec(
            num_scalar_prefetch=3,
            grid=(steps,),
            in_specs=picks + picks + [whole, whole],
            out_specs=(whole, whole),
            scratch_shapes=[pltpu.VMEM((rows, width), jnp.float32)] * 2,
        ),
        compiler_params=pltpu.CompilerParams(vmem_limit_bytes=60 * 2**20),
        cost_estimate=pl.CostEstimate(
            flops=4 * 10**9, bytes_accessed=16 * 2**20, transcendentals=3 * 10**6
        ),
        name="key_side",
    )(qi, ki, on, *[q_all] * nb, *[c_all] * nb, k, v)


def key_plan(far, treated, me, nb):
    total = far.shape[0]
    mine = (far // nb) == me
    ids = jnp.arange(total)
    rank = jnp.sum((ids[None, :] < ids[:, None]) & mine[None, :], axis=1)
    hit = mine[None, :] & (rank[None, :] == jnp.arange(nb * FAR)[:, None])
    flag = jnp.sum(
        jnp.where(far[:, None] == jnp.arange(treated.shape[0])[None, :], treated[None, :], 0),
        axis=1,
    )

    def take(values):
        return jnp.sum(jnp.where(hit, values[None, :], 0), axis=1)

    local = jnp.arange(nb)
    after = me * nb + local + 1
    last = treated.shape[0] - 1
    qi = jnp.concatenate([me * nb + local, jnp.minimum(after, last), take(ids // FAR)])
    ki = jnp.concatenate([local, local, take(far % nb)])
    on = jnp.concatenate(
        [jnp.full((nb,), 2), (after <= last).astype(jnp.int32), take(flag)]
    )
    return qi.astype(jnp.int32), ki.astype(jnp.int32), on.astype(jnp.int32)


def places():
    me = lax.axis_index("seq")
    x, y = (me // 2) % 2, (me // 4) % 2
    side = me + 1 - 2 * (me % 2)
    over_x = 2 - 4 * x
    over_y = 4 - 8 * y
    return me, side, me + over_x, me + over_y, me + over_x + over_y


def greet(peers):
    barrier = pltpu.get_barrier_semaphore()
    for peer in peers:
        pl.semaphore_signal(barrier, inc=1, device_id=peer, device_id_type=pl.DeviceIdType.MESH)
    pl.semaphore_wait(barrier, len(peers))


class Spread:
    def __init__(self, src, dst, send, recv, own):
        self.src, self.dst, self.send, self.recv, self.own = src, dst, send, recv, own
        self.me, self.side, self.px, self.py, self.pd = places()
        self.rows = src.shape[0]
        self.step = self.rows // CHUNKS
        self.sent = []

    def slot(self, origin, j):
        return self.dst.at[pl.ds(pl.multiple_of(origin * self.rows, self.rows) + j * self.step, self.step)]

    def copy(self, src, origin, kind, j, to):
        return pltpu.make_async_remote_copy(
            src_ref=src,
            dst_ref=self.slot(origin, j),
            send_sem=self.send.at[kind, j],
            recv_sem=self.recv.at[kind, j],
            device_id={"seq": to},
            device_id_type=pl.DeviceIdType.MESH,
        )

    def push(self, src, origin, kind, j, to):
        made = self.copy(src, origin, kind, j, to)
        made.start()
        self.sent.append(made)

    def take(self, origin, kind, j):
        self.copy(self.slot(origin, j), origin, kind, j, self.side).wait_recv()

    def begin(self):
        self.keep = pltpu.make_async_copy(
            self.src,
            self.dst.at[pl.ds(pl.multiple_of(self.me * self.rows, self.rows), self.rows)],
            self.own,
        )
        half = CHUNKS // 2
        for n in range(CHUNKS):
            j, i = n, (n + half) % CHUNKS
            self.push(self.src.at[pl.ds(j * self.step, self.step)], self.me, 0, j, self.px)
            self.push(self.src.at[pl.ds(i * self.step, self.step)], self.me, 1, i, self.py)
        for j in range(CHUNKS):
            self.push(self.src.at[pl.ds(j * self.step, self.step)], self.me, 3, j, self.side)
        self.keep.start()

    def relay(self):
        half = CHUNKS // 2
        for n in range(CHUNKS):
            j, i = n, (n + half) % CHUNKS
            self.take(self.px, 0, j)
            if n < half:
                self.push(self.slot(self.px, j), self.px, 2, j, self.py)
            self.push(self.slot(self.px, j), self.px, 4, j, self.side)
            self.take(self.py, 1, i)
            if n < half:
                self.push(self.slot(self.py, i), self.py, 2, i, self.px)
            self.push(self.slot(self.py, i), self.py, 5, i, self.side)

    def finish(self):
        half = CHUNKS // 2
        for n in range(half):
            for j in (n, n + half):
                self.take(self.pd, 2, j)
                self.push(self.slot(self.pd, j), self.pd, 6, j, self.side)

    def drain(self):
        far = self.side - self.me
        for kind, origin in ((3, self.me), (4, self.px), (5, self.py), (6, self.pd)):
            for j in range(CHUNKS):
                self.take(origin + far, kind, j)
        for made in self.sent:
            made.wait_send()
        self.keep.wait()


def seq_peers():
    _, side, px, py, pd = places()
    return [{"seq": p} for p in (side, px, py, pd)]


def spread_kernel(count, *refs):
    srcs, later = refs[:count], refs[count]
    dsts, later_out = refs[count + 1 : 2 * count + 1], refs[2 * count + 1]
    send, recv, own = refs[2 * count + 2 :]
    greet(seq_peers())
    passed = pltpu.make_async_copy(later, later_out, own.at[count])
    passed.start()
    jobs = [
        Spread(srcs[a], dsts[a], send.at[a], recv.at[a], own.at[a]) for a in range(count)
    ]
    for job in jobs:
        job.begin()
    for job in jobs:
        job.relay()
    for job in jobs:
        job.finish()
    for job in jobs:
        job.drain()
    passed.wait()


def spread(arrays, later, ident):
    count = len(arrays)
    rows, width = arrays[0].shape
    anywhere = pl.BlockSpec(memory_space=pl.ANY)
    full = jax.ShapeDtypeStruct((SEQS * rows, width), jnp.bfloat16)
    return pl.pallas_call(
        functools.partial(spread_kernel, count),
        out_shape=(full,) * count + (jax.ShapeDtypeStruct(later.shape, later.dtype),),
        in_specs=[anywhere] * (count + 1),
        out_specs=(anywhere,) * (count + 1),
        scratch_shapes=[
            pltpu.SemaphoreType.DMA((count, 7, CHUNKS)),
            pltpu.SemaphoreType.DMA((count, 7, CHUNKS)),
            pltpu.SemaphoreType.DMA((count + 1,)),
        ],
        compiler_params=pltpu.CompilerParams(collective_id=ident, has_side_effects=True, vmem_limit_bytes=60 * 2**20),
        name="spread_rows",
    )(*arrays, later)


def tail_kernel(
    c_ref, gw_ref, dg_ref, c_all, gw_out, dg_out,
    got_side, mid, got_z, low, got_xy, dg_side, dg_z, dg_yx,
    send, recv, own, red_send, red_recv,
):
    greet(seq_peers() + [{"dp": lax.rem(lax.axis_index("dp") + k, DPS)} for k in range(1, DPS)])
    me, side, px, py, pd = places()
    core = me % 2
    z = lax.axis_index("dp")
    yx = me // 2
    job = Spread(c_ref, c_all, send, recv, own)
    sent = []

    def push(src, dst, at, to):
        made = pltpu.make_async_remote_copy(
            src_ref=src, dst_ref=dst, send_sem=red_send.at[at], recv_sem=red_recv.at[at],
            device_id=to, device_id_type=pl.DeviceIdType.MESH,
        )
        made.start()
        sent.append(made)
        return made

    one = push(gw_ref.at[1 - core], got_side, 0, {"seq": side})
    dg_one = push(dg_ref, dg_side, 1, {"seq": side})
    job.begin()
    one.wait_recv()
    dg_one.wait_recv()
    for p in range(DPS):
        mid[p] = (
            gw_ref[core, p].astype(jnp.float32) + got_side[p].astype(jnp.float32)
        ).astype(jnp.bfloat16)
    dg_z[z] = dg_ref[...] + dg_side[...]
    twos = []
    for k in range(1, DPS):
        to = lax.rem(z + k, DPS)
        twos.append(push(mid.at[to], got_z.at[k - 1], 2 * k, {"dp": to}))
        twos.append(push(dg_z.at[z], dg_z.at[z], 2 * k + 1, {"dp": to}))
    job.relay()
    for two in twos:
        two.wait_recv()
    total = gw_ref[core, z].astype(jnp.float32) + got_side[z].astype(jnp.float32)
    for k in range(DPS - 1):
        total += got_z[k].astype(jnp.float32)
    low[...] = total.astype(jnp.bfloat16).reshape(low.shape)
    dg_yx[yx] = dg_z[0] + dg_z[1] + dg_z[2] + dg_z[3]
    threes = []
    for k, to in enumerate((px, py, pd)):
        threes.append(push(low.at[to // 2], got_xy.at[k], 8 + 2 * k, {"seq": to}))
        threes.append(push(dg_yx.at[yx], dg_yx.at[yx], 9 + 2 * k, {"seq": to}))
    job.finish()
    for three in threes:
        three.wait_recv()
    result = low[yx].astype(jnp.float32)
    for k in range(3):
        result += got_xy[k].astype(jnp.float32)
    gw_out[...] = result
    dg_out[...] = dg_yx[0] + dg_yx[1] + dg_yx[2] + dg_yx[3]
    job.drain()
    for made in sent:
        made.wait_send()


def tail(c, gw, dg):
    rows, width = c.shape
    depth = width // (SEQS * DPS)
    anywhere = pl.BlockSpec(memory_space=pl.ANY)
    vmem = pl.BlockSpec(memory_space=pltpu.VMEM)
    part = (SEQS // 2) * depth
    b16 = jnp.bfloat16
    return pl.pallas_call(
        tail_kernel,
        out_shape=(
            jax.ShapeDtypeStruct((SEQS * rows, width), b16),
            jax.ShapeDtypeStruct((depth, width), jnp.float32),
            jax.ShapeDtypeStruct(dg.shape, jnp.float32),
        ),
        in_specs=[anywhere, vmem, vmem],
        out_specs=(anywhere, vmem, vmem),
        scratch_shapes=[
            pltpu.VMEM((DPS, part, width), b16),
            pltpu.VMEM((DPS, part, width), b16),
            pltpu.VMEM((DPS - 1, part, width), b16),
            pltpu.VMEM((SEQS // 2, depth, width), b16),
            pltpu.VMEM((3, depth, width), b16),
            pltpu.VMEM(dg.shape, jnp.float32),
            pltpu.VMEM((DPS,) + dg.shape, jnp.float32),
            pltpu.VMEM((SEQS // 2,) + dg.shape, jnp.float32),
            pltpu.SemaphoreType.DMA((7, CHUNKS)),
            pltpu.SemaphoreType.DMA((7, CHUNKS)),
            pltpu.SemaphoreType.DMA,
            pltpu.SemaphoreType.DMA((14,)),
            pltpu.SemaphoreType.DMA((14,)),
        ],
        compiler_params=pltpu.CompilerParams(
            collective_id=2, has_side_effects=True, vmem_limit_bytes=60 * 2**20
        ),
        name="tail_exchange",
    )(c, gw, dg)


def gather(rows):
    return lax.all_gather(rows, "seq", axis=0, tiled=True)


def body(q, k, v, gate, cot, far_blocks, treated, gain, w):
    q, k, v, gate, cot = q[0], k[0], v[0], gate[0], cot[0]
    rows, width = q.shape
    nb = rows // BLK
    me = lax.axis_index("seq").astype(jnp.int32)
    far = far_blocks[0].reshape(-1)
    flags = treated[0]
    seqs, dps = lax.axis_size("seq"), lax.axis_size("dp")
    direct = (seqs, dps) == (SEQS, DPS)
    if direct:
        k_all, v_all, q_late = spread([k, v], q, 1)
        q_all = gather(q_late)
    else:
        k_all, v_all, q_all = gather(k), gather(v), gather(q)
    out, dq, dgate, mixed, c, dgain = run_query(
        q, k, v, k_all, v_all, gate, cot, far, flags, me[None], gain[None], w
    )
    grad_weight = dot(mixed, cot, TN)
    if direct:
        parts = grad_weight.astype(jnp.bfloat16).reshape(seqs // 2, 2, dps, -1, width)
        parts = parts.transpose(1, 2, 0, 3, 4).reshape(2, dps, -1, width)
        c_all, grad_weight, dgain = tail(c, parts, dgain)
        dgain = jnp.sum(dgain, axis=0)
    else:
        c_all = gather(c)
        grad_weight = lax.psum_scatter(grad_weight, ("seq", "dp"), scatter_dimension=0, tiled=True)
        dgain = lax.psum(jnp.sum(dgain, axis=0), ("seq", "dp"))
    qi, ki, on = key_plan(far, flags, me, nb)
    dk, dv = run_keys(qi, ki, on, q_all, c_all, k, v)
    return out[None], dq[None], dk[None], dv[None], dgate[None], grad_weight, dgain


def solution(mesh):
    big = P("dp", "seq", None)
    in_specs = (big,) * 5 + (P("dp", None, None), P("dp", None), P(), P())
    out_specs = (big,) * 5 + (P(("seq", "dp"), None), P())
    return jax.shard_map(body, mesh=mesh, in_specs=in_specs, out_specs=out_specs, check_vma=False)
```

```python
import functools

import jax
import jax.numpy as jnp
from jax import lax
from jax.experimental import pallas as pl
from jax.experimental.pallas import tpu as pltpu
from jax.sharding import PartitionSpec as P

HEADS = 8
HEAD_DIM = 128
BLK = 128
FAR = 4
EPS = 1e-05
CHUNKS = 4
GROUP = 4
SEQS, DPS = 8, 4
SCALE = HEAD_DIM ** (-0.5)
NT = (((1,), (1,)), ((), ()))
TN = (((0,), (0,)), ((), ()))


def dot(a, b, dims=(((1,), (0,)), ((), ()))):
    return lax.dot_general(a, b, dims, preferred_element_type=jnp.float32)


def silu_parts(raw):
    half = raw * (0.5 * SCALE)
    t = jnp.tanh(half)
    act = half + half * t
    sig = 0.5 + 0.5 * t
    return act, sig + act * (1.0 - sig)


def query_kernel(
    nb, far_s, treated_s, my_s, q_ref, k0, v0, k1, v1, k2, v2, k3, v3, k4, v4, k5, v5,
    gate_ref, cot_ref, gain_ref, w_ref,
    out_ref, dq_ref, dgate_ref, mixed_ref, c_ref, dgain_ref, att, slope, vals, keys,
):
    i = pl.program_id(0)
    block = my_s[0] * nb + i
    flags = [None, (block > 0).astype(jnp.float32)]
    flags += [treated_s[far_s[block * FAR + f]].astype(jnp.float32) for f in range(FAR)]
    for p, (one_k, one_v) in enumerate(zip((k0, k1, k2, k3, k4, k5), (v0, v1, v2, v3, v4, v5))):
        at = slice(p * BLK, (p + 1) * BLK)
        keys[at] = one_k[...]
        vals[at] = one_v[...] if p == 0 else one_v[...] * flags[p].astype(jnp.bfloat16)
    row = lax.broadcasted_iota(jnp.int32, (BLK, BLK), 0)
    col = lax.broadcasted_iota(jnp.int32, (BLK, BLK), 1)
    tril = (row >= col).astype(jnp.float32)
    for h in range(HEADS):
        hs = slice(h * HEAD_DIM, (h + 1) * HEAD_DIM)
        q = q_ref[:, hs]
        act, der = silu_parts(dot(q, keys[:, hs], NT))
        act = jnp.concatenate([act[:, :BLK] * tril, act[:, BLK:]], axis=1)
        slope[h, :, :BLK] = der[:, :BLK] * tril
        slope[h, :, BLK:] = der[:, BLK:]
        att[:, hs] = dot(act.astype(jnp.bfloat16), vals[:, hs])
    attention = att[...]
    centered = attention - jnp.mean(attention, axis=1, keepdims=True)
    inv_std = lax.rsqrt(jnp.mean(centered * centered, axis=1, keepdims=True) + EPS)
    normed = centered * inv_std
    gate = gate_ref[...].astype(jnp.float32)
    gain = gain_ref[...]
    mixed = (normed * gain * gate).astype(jnp.bfloat16)
    mixed_ref[...] = mixed
    out_ref[...] = dot(mixed, w_ref[...]).astype(jnp.bfloat16)
    gm = dot(cot_ref[...], w_ref[...], NT)
    dgate_ref[...] = (gm * normed * gain).astype(jnp.bfloat16)
    scaled = gm * gate
    part = jnp.sum((scaled * normed).reshape(BLK // 8, 8, -1), axis=0)

    @pl.when(i == 0)
    def _():
        dgain_ref[...] = part

    @pl.when(i > 0)
    def _():
        dgain_ref[...] += part

    g = scaled * gain
    c = inv_std * (
        g - jnp.mean(g, axis=1, keepdims=True)
        - normed * jnp.mean(g * normed, axis=1, keepdims=True)
    )
    c_ref[...] = c.astype(jnp.bfloat16)
    for h in range(HEADS):
        hs = slice(h * HEAD_DIM, (h + 1) * HEAD_DIM)
        ch = c_ref[:, hs]
        ds = dot(ch, vals[:, hs], NT) * slope[h]
        dq = dot(ds.astype(jnp.bfloat16), keys[:, hs])
        dq_ref[:, hs] = (dq * SCALE).astype(jnp.bfloat16)


def key_kernel(nb, steps, qi_s, ki_s, on_s, *refs):
    q_refs, c_refs = refs[:nb], refs[nb : 2 * nb]
    k_ref, v_ref, dk_ref, dv_ref, dk_acc, dv_acc = refs[2 * nb :]
    r = pl.program_id(0)
    row = lax.broadcasted_iota(jnp.int32, (BLK, BLK), 0)
    col = lax.broadcasted_iota(jnp.int32, (BLK, BLK), 1)
    upper = (col >= row).astype(jnp.float32)

    @pl.when(r == 0)
    def _():
        for n in range(nb):
            at = slice(n * BLK, (n + 1) * BLK)
            for h in range(HEADS):
                hs = slice(h * HEAD_DIM, (h + 1) * HEAD_DIM)
                q, c = q_refs[n][:, hs], c_refs[n][:, hs]
                act, der = silu_parts(dot(k_ref[at, hs], q, NT))
                da = dot(v_ref[at, hs], c, NT)
                dv_acc[at, hs] = dot((act * upper).astype(jnp.bfloat16), c)
                dk_acc[at, hs] = dot((da * der * upper).astype(jnp.bfloat16), q)

    @pl.when(r > 0)
    def _():
        for n in range(nb):
            at = pl.ds(pl.multiple_of(ki_s[r * nb + n] * BLK, BLK), BLK)
            on = (on_s[r * nb + n] > 0).astype(jnp.bfloat16)
            for first in range(0, HEADS, GROUP):
                cuts = [
                    slice(h * HEAD_DIM, (h + 1) * HEAD_DIM) for h in range(first, first + GROUP)
                ]
                qs = [q_refs[n][:, hs] for hs in cuts]
                cs = [c_refs[n][:, hs] * on for hs in cuts]
                raw = [dot(k_ref[at, hs], q, NT) for hs, q in zip(cuts, qs)]
                da = [dot(v_ref[at, hs], c, NT) for hs, c in zip(cuts, cs)]
                act, der = silu_parts(jnp.concatenate(raw, axis=1))
                ds = (jnp.concatenate(da, axis=1) * der).astype(jnp.bfloat16)
                act = act.astype(jnp.bfloat16)
                dv = [dot(act[:, g * BLK : (g + 1) * BLK], cs[g]) for g in range(GROUP)]
                dk = [dot(ds[:, g * BLK : (g + 1) * BLK], qs[g]) for g in range(GROUP)]
                wide = slice(first * HEAD_DIM, (first + GROUP) * HEAD_DIM)
                dv_acc[at, wide] += jnp.concatenate(dv, axis=1)
                dk_acc[at, wide] += jnp.concatenate(dk, axis=1)

    @pl.when(r == steps - 1)
    def _():
        dk_ref[...] = (dk_acc[...] * SCALE).astype(jnp.bfloat16)
        dv_ref[...] = dv_acc[...].astype(jnp.bfloat16)


def run_query(q, k, v, k_all, v_all, gate, cot, far, treated, me, gain, w):
    rows, width = q.shape
    nb = rows // BLK
    shape = (BLK, width)
    own = pl.BlockSpec(shape, lambda i, far, tr, my: (i, 0))
    prev = pl.BlockSpec(shape, lambda i, far, tr, my: (jnp.maximum(my[0] * nb + i - 1, 0), 0))

    def listed(f):
        return pl.BlockSpec(shape, lambda i, far, tr, my: (far[(my[0] * nb + i) * FAR + f], 0))

    kv_specs = [own, own, prev, prev]
    kv = [k, v, k_all, v_all]
    for f in range(FAR):
        kv_specs += [listed(f)] * 2
        kv += [k_all, v_all]
    whole = pl.BlockSpec((width, width), lambda i, far, tr, my: (0, 0))
    vec = pl.BlockSpec((1, width), lambda i, far, tr, my: (0, 0))
    vec8 = pl.BlockSpec((8, width), lambda i, far, tr, my: (0, 0))
    big = jax.ShapeDtypeStruct((rows, width), jnp.bfloat16)
    return pl.pallas_call(
        functools.partial(query_kernel, nb),
        out_shape=(big, big, big, big, big, jax.ShapeDtypeStruct((8, width), jnp.float32)),
        grid_spec=pltpu.PrefetchScalarGridSpec(
            num_scalar_prefetch=3,
            grid=(nb,),
            in_specs=[own] + kv_specs + [own, own, vec, whole],
            out_specs=(own, own, own, own, own, vec8),
            scratch_shapes=[
                pltpu.VMEM((BLK, width), jnp.float32),
                pltpu.VMEM((HEADS, BLK, (2 + FAR) * BLK), jnp.float32),
                pltpu.VMEM(((2 + FAR) * BLK, width), jnp.bfloat16),
                pltpu.VMEM(((2 + FAR) * BLK, width), jnp.bfloat16),
            ],
        ),
        compiler_params=pltpu.CompilerParams(vmem_limit_bytes=60 * 2**20),
        cost_estimate=pl.CostEstimate(
            flops=8 * 10**9, bytes_accessed=24 * 2**20, transcendentals=3 * 10**6
        ),
        name="query_side",
    )(far, treated, me, q, *kv, gate, cot, gain, w)


def run_keys(qi, ki, on, q_all, c_all, k, v):
    rows, width = k.shape
    nb = rows // BLK
    steps = qi.shape[0] // nb

    def pick(n):
        return pl.BlockSpec((BLK, width), lambda r, qi, ki, on: (qi[r * nb + n], 0))

    picks = [pick(n) for n in range(nb)]
    whole = pl.BlockSpec((rows, width), lambda r, qi, ki, on: (0, 0))
    big = jax.ShapeDtypeStruct((rows, width), jnp.bfloat16)
    return pl.pallas_call(
        functools.partial(key_kernel, nb, steps),
        out_shape=(big, big),
        grid_spec=pltpu.PrefetchScalarGridSpec(
            num_scalar_prefetch=3,
            grid=(steps,),
            in_specs=picks + picks + [whole, whole],
            out_specs=(whole, whole),
            scratch_shapes=[pltpu.VMEM((rows, width), jnp.float32)] * 2,
        ),
        compiler_params=pltpu.CompilerParams(vmem_limit_bytes=60 * 2**20),
        cost_estimate=pl.CostEstimate(
            flops=4 * 10**9, bytes_accessed=16 * 2**20, transcendentals=3 * 10**6
        ),
        name="key_side",
    )(qi, ki, on, *[q_all] * nb, *[c_all] * nb, k, v)


def key_plan(far, treated, me, nb):
    total = far.shape[0]
    mine = (far // nb) == me
    ids = jnp.arange(total)
    rank = jnp.sum((ids[None, :] < ids[:, None]) & mine[None, :], axis=1)
    hit = mine[None, :] & (rank[None, :] == jnp.arange(nb * FAR)[:, None])
    flag = jnp.sum(
        jnp.where(far[:, None] == jnp.arange(treated.shape[0])[None, :], treated[None, :], 0),
        axis=1,
    )

    def take(values):
        return jnp.sum(jnp.where(hit, values[None, :], 0), axis=1)

    local = jnp.arange(nb)
    after = me * nb + local + 1
    last = treated.shape[0] - 1
    qi = jnp.concatenate([me * nb + local, jnp.minimum(after, last), take(ids // FAR)])
    ki = jnp.concatenate([local, local, take(far % nb)])
    on = jnp.concatenate(
        [jnp.full((nb,), 2), (after <= last).astype(jnp.int32), take(flag)]
    )
    return qi.astype(jnp.int32), ki.astype(jnp.int32), on.astype(jnp.int32)


def places():
    me = lax.axis_index("seq")
    x, y = (me // 2) % 2, (me // 4) % 2
    side = me + 1 - 2 * (me % 2)
    over_x = 2 - 4 * x
    over_y = 4 - 8 * y
    return me, side, me + over_x, me + over_y, me + over_x + over_y


def greet(peers):
    barrier = pltpu.get_barrier_semaphore()
    for peer in peers:
        pl.semaphore_signal(barrier, inc=1, device_id=peer, device_id_type=pl.DeviceIdType.MESH)
    pl.semaphore_wait(barrier, len(peers))


class Spread:
    def __init__(self, src, dst, send, recv, own):
        self.src, self.dst, self.send, self.recv, self.own = src, dst, send, recv, own
        self.me, self.side, self.px, self.py, self.pd = places()
        self.rows = src.shape[0]
        self.step = self.rows // CHUNKS
        self.sent = []

    def slot(self, origin, j):
        return self.dst.at[pl.ds(pl.multiple_of(origin * self.rows, self.rows) + j * self.step, self.step)]

    def copy(self, src, origin, kind, j, to):
        return pltpu.make_async_remote_copy(
            src_ref=src,
            dst_ref=self.slot(origin, j),
            send_sem=self.send.at[kind, j],
            recv_sem=self.recv.at[kind, j],
            device_id={"seq": to},
            device_id_type=pl.DeviceIdType.MESH,
        )

    def push(self, src, origin, kind, j, to):
        made = self.copy(src, origin, kind, j, to)
        made.start()
        self.sent.append(made)

    def take(self, origin, kind, j):
        self.copy(self.slot(origin, j), origin, kind, j, self.side).wait_recv()

    def begin(self):
        self.keep = pltpu.make_async_copy(
            self.src,
            self.dst.at[pl.ds(pl.multiple_of(self.me * self.rows, self.rows), self.rows)],
            self.own,
        )
        half = CHUNKS // 2
        for n in range(CHUNKS):
            j, i = n, (n + half) % CHUNKS
            self.push(self.src.at[pl.ds(j * self.step, self.step)], self.me, 0, j, self.px)
            self.push(self.src.at[pl.ds(i * self.step, self.step)], self.me, 1, i, self.py)
        for j in range(CHUNKS):
            self.push(self.src.at[pl.ds(j * self.step, self.step)], self.me, 3, j, self.side)
        self.keep.start()

    def relay(self):
        half = CHUNKS // 2
        for n in range(CHUNKS):
            j, i = n, (n + half) % CHUNKS
            self.take(self.px, 0, j)
            if n < half:
                self.push(self.slot(self.px, j), self.px, 2, j, self.py)
            self.push(self.slot(self.px, j), self.px, 4, j, self.side)
            self.take(self.py, 1, i)
            if n < half:
                self.push(self.slot(self.py, i), self.py, 2, i, self.px)
            self.push(self.slot(self.py, i), self.py, 5, i, self.side)

    def finish(self):
        half = CHUNKS // 2
        for n in range(half):
            for j in (n, n + half):
                self.take(self.pd, 2, j)
                self.push(self.slot(self.pd, j), self.pd, 6, j, self.side)

    def drain(self):
        far = self.side - self.me
        for kind, origin in ((3, self.me), (4, self.px), (5, self.py), (6, self.pd)):
            for j in range(CHUNKS):
                self.take(origin + far, kind, j)
        for made in self.sent:
            made.wait_send()
        self.keep.wait()


def seq_peers():
    _, side, px, py, pd = places()
    return [{"seq": p} for p in (side, px, py, pd)]


def spread_kernel(count, *refs):
    srcs, dsts = refs[:count], refs[count : 2 * count]
    send, recv, own = refs[2 * count :]
    greet(seq_peers())
    jobs = [
        Spread(srcs[a], dsts[a], send.at[a], recv.at[a], own.at[a]) for a in range(count)
    ]
    for job in jobs:
        job.begin()
    for job in jobs:
        job.relay()
    for job in jobs:
        job.finish()
    for job in jobs:
        job.drain()


def spread(arrays, ident):
    count = len(arrays)
    rows, width = arrays[0].shape
    anywhere = pl.BlockSpec(memory_space=pl.ANY)
    full = jax.ShapeDtypeStruct((SEQS * rows, width), jnp.bfloat16)
    return pl.pallas_call(
        functools.partial(spread_kernel, count),
        out_shape=(full,) * count,
        in_specs=[pl.BlockSpec(memory_space=pltpu.VMEM)] * count,
        out_specs=(anywhere,) * count,
        scratch_shapes=[
            pltpu.SemaphoreType.DMA((count, 7, CHUNKS)),
            pltpu.SemaphoreType.DMA((count, 7, CHUNKS)),
            pltpu.SemaphoreType.DMA((count,)),
        ],
        compiler_params=pltpu.CompilerParams(collective_id=ident, has_side_effects=True, vmem_limit_bytes=60 * 2**20),
        name="spread_rows",
    )(*arrays)


def tail_kernel(
    c_ref, gw_ref, dg_ref, c_all, gw_out, dg_out,
    got_side, mid, got_z, low, got_xy, dg_side, dg_z, dg_yx,
    send, recv, own, red_send, red_recv,
):
    greet(seq_peers() + [{"dp": lax.rem(lax.axis_index("dp") + k, DPS)} for k in range(1, DPS)])
    me, side, px, py, pd = places()
    core = me % 2
    z = lax.axis_index("dp")
    yx = me // 2
    job = Spread(c_ref, c_all, send, recv, own)
    sent = []

    def push(src, dst, at, to):
        made = pltpu.make_async_remote_copy(
            src_ref=src, dst_ref=dst, send_sem=red_send.at[at], recv_sem=red_recv.at[at],
            device_id=to, device_id_type=pl.DeviceIdType.MESH,
        )
        made.start()
        sent.append(made)
        return made

    one = push(gw_ref.at[1 - core], got_side, 0, {"seq": side})
    dg_one = push(dg_ref, dg_side, 1, {"seq": side})
    job.begin()
    one.wait_recv()
    dg_one.wait_recv()
    for p in range(DPS):
        mid[p] = (
            gw_ref[core, p].astype(jnp.float32) + got_side[p].astype(jnp.float32)
        ).astype(jnp.bfloat16)
    dg_z[z] = dg_ref[...] + dg_side[...]
    twos = []
    for k in range(1, DPS):
        to = lax.rem(z + k, DPS)
        twos.append(push(mid.at[to], got_z.at[k - 1], 2 * k, {"dp": to}))
        twos.append(push(dg_z.at[z], dg_z.at[z], 2 * k + 1, {"dp": to}))
    job.relay()
    for two in twos:
        two.wait_recv()
    total = gw_ref[core, z].astype(jnp.float32) + got_side[z].astype(jnp.float32)
    for k in range(DPS - 1):
        total += got_z[k].astype(jnp.float32)
    low[...] = total.astype(jnp.bfloat16).reshape(low.shape)
    dg_yx[yx] = dg_z[0] + dg_z[1] + dg_z[2] + dg_z[3]
    threes = []
    for k, to in enumerate((px, py, pd)):
        threes.append(push(low.at[to // 2], got_xy.at[k], 8 + 2 * k, {"seq": to}))
        threes.append(push(dg_yx.at[yx], dg_yx.at[yx], 9 + 2 * k, {"seq": to}))
    job.finish()
    for three in threes:
        three.wait_recv()
    result = low[yx].astype(jnp.float32)
    for k in range(3):
        result += got_xy[k].astype(jnp.float32)
    gw_out[...] = result
    dg_out[...] = dg_yx[0] + dg_yx[1] + dg_yx[2] + dg_yx[3]
    job.drain()
    for made in sent:
        made.wait_send()


def tail(c, gw, dg):
    rows, width = c.shape
    depth = width // (SEQS * DPS)
    anywhere = pl.BlockSpec(memory_space=pl.ANY)
    vmem = pl.BlockSpec(memory_space=pltpu.VMEM)
    part = (SEQS // 2) * depth
    b16 = jnp.bfloat16
    return pl.pallas_call(
        tail_kernel,
        out_shape=(
            jax.ShapeDtypeStruct((SEQS * rows, width), b16),
            jax.ShapeDtypeStruct((depth, width), jnp.float32),
            jax.ShapeDtypeStruct(dg.shape, jnp.float32),
        ),
        in_specs=[vmem, vmem, vmem],
        out_specs=(anywhere, vmem, vmem),
        scratch_shapes=[
            pltpu.VMEM((DPS, part, width), b16),
            pltpu.VMEM((DPS, part, width), b16),
            pltpu.VMEM((DPS - 1, part, width), b16),
            pltpu.VMEM((SEQS // 2, depth, width), b16),
            pltpu.VMEM((3, depth, width), b16),
            pltpu.VMEM(dg.shape, jnp.float32),
            pltpu.VMEM((DPS,) + dg.shape, jnp.float32),
            pltpu.VMEM((SEQS // 2,) + dg.shape, jnp.float32),
            pltpu.SemaphoreType.DMA((7, CHUNKS)),
            pltpu.SemaphoreType.DMA((7, CHUNKS)),
            pltpu.SemaphoreType.DMA,
            pltpu.SemaphoreType.DMA((14,)),
            pltpu.SemaphoreType.DMA((14,)),
        ],
        compiler_params=pltpu.CompilerParams(
            collective_id=2, has_side_effects=True, vmem_limit_bytes=60 * 2**20
        ),
        name="tail_exchange",
    )(c, gw, dg)


def gather(rows):
    return lax.all_gather(rows, "seq", axis=0, tiled=True)


def body(q, k, v, gate, cot, far_blocks, treated, gain, w):
    q, k, v, gate, cot = q[0], k[0], v[0], gate[0], cot[0]
    rows, width = q.shape
    nb = rows // BLK
    me = lax.axis_index("seq").astype(jnp.int32)
    far = far_blocks[0].reshape(-1)
    flags = treated[0]
    seqs, dps = lax.axis_size("seq"), lax.axis_size("dp")
    direct = (seqs, dps) == (SEQS, DPS)
    if direct:
        k_all, v_all = spread([k, v], 1)
        q_late, k_all, v_all = lax.optimization_barrier((q, k_all, v_all))
        q_all = gather(q_late)
    else:
        k_all, v_all, q_all = gather(k), gather(v), gather(q)
    out, dq, dgate, mixed, c, dgain = run_query(
        q, k, v, k_all, v_all, gate, cot, far, flags, me[None], gain[None], w
    )
    grad_weight = dot(mixed, cot, TN)
    if direct:
        parts = grad_weight.astype(jnp.bfloat16).reshape(seqs // 2, 2, dps, -1, width)
        parts = parts.transpose(1, 2, 0, 3, 4).reshape(2, dps, -1, width)
        c_all, grad_weight, dgain = tail(c, parts, dgain)
        dgain = jnp.sum(dgain, axis=0)
    else:
        c_all = gather(c)
        grad_weight = lax.psum_scatter(grad_weight, ("seq", "dp"), scatter_dimension=0, tiled=True)
        dgain = lax.psum(jnp.sum(dgain, axis=0), ("seq", "dp"))
    qi, ki, on = key_plan(far, flags, me, nb)
    dk, dv = run_keys(qi, ki, on, q_all, c_all, k, v)
    return out[None], dq[None], dk[None], dv[None], dgate[None], grad_weight, dgain


def solution(mesh):
    big = P("dp", "seq", None)
    in_specs = (big,) * 5 + (P("dp", None, None), P("dp", None), P(), P())
    out_specs = (big,) * 5 + (P(("seq", "dp"), None), P())
    return jax.shard_map(body, mesh=mesh, in_specs=in_specs, out_specs=out_specs, check_vma=False)
```
